32 devices in a mesh: heads: 4 (over z), keys: 8 (over y, x, core).
Axes of the slice: x: 2, y: 2, z: 4, core: 2. Of those that a mesh axis runs over, the one named last changes fastest.
Arguments:
- queries: bfloat16 [2048, 4096], P('keys', 'heads')
- key_states: bfloat16 [65536, 4096], P('keys', 'heads')
- value_states: bfloat16 [65536, 4096], P('keys', 'heads'), may hold values from -6 to 6
- block_ids: int32 [32, 768], P('heads', 'keys'), may hold values from 0 to 1023, as said below
- block_counts: int32 [32, 8], P('heads', 'keys'), may hold values from 2 to 96, as said below
- out_weight: bfloat16 [4096, 4096], P('heads'), may hold values from -0.09375 to 0.09375
Outputs:
- projected: bfloat16 [2048, 4096], P('keys', 'heads')
The draws below stay inside these ranges and needn't reach their ends.
Inputs may be any that keep to these rules, and one draw needn't show every extreme that they name: `block_ids`: entry h, r * 96 + j names query block b // 64 and tile b % 64 of key range r for head h; the first block_counts[h, r] entries of a head and key range are distinct, the rest are ignored; every query block is named by a counted entry of every head. `block_counts`: some head and key range has exactly 96 counted entries.
All inputs are finite; a program needn't handle non-finite values.
Results may differ from the reference program's by a relative error of at most 0.025.
Values may be sent and summed in bfloat16 or wider, within the bound.
A program may use at most 192 MiB of HBM per device.

```python
import jax
import jax.numpy as jnp
from jax import lax

HEADS = 32
HEAD_DIM = 128
D = 4096
BLOCK = 128
Q_LEN = 2048
CTX = 65536
QBLOCKS = 16
KTILES = 64
LBLK = 1024
CAP = 96
COVER = 2
N_KEYS = 8


def listed_blocks(key):
    high_count = jax.random.randint(jax.random.fold_in(key, 101), (HEADS, 1), max(COVER, CAP // 10), CAP + 1)
    low_count = jnp.maximum(COVER, high_count // 2)
    raw_draw = jax.random.randint(jax.random.fold_in(key, 102), (HEADS, N_KEYS), 0, 1 << 20)
    counts = low_count + raw_draw % (high_count - low_count + 1)
    full_head = jax.random.randint(jax.random.fold_in(key, 103), (), 0, HEADS)
    full_range = jax.random.randint(jax.random.fold_in(key, 104), (), 0, N_KEYS)
    counts = counts.at[full_head, full_range].set(CAP)
    slot_keys = jax.random.split(jax.random.fold_in(key, 105), HEADS * N_KEYS)
    ranges = jnp.tile(jnp.arange(N_KEYS, dtype=jnp.int32), HEADS)

    def one_list(slot_key, range_index):
        cover_tile = jax.random.randint(jax.random.fold_in(slot_key, 1), (COVER,), 0, KTILES)
        cover_query = (range_index + jnp.arange(COVER, dtype=jnp.int32) * N_KEYS) % QBLOCKS
        cover_ids = (cover_query * KTILES + cover_tile).astype(jnp.int32)
        shuffled = jax.random.permutation(jax.random.fold_in(slot_key, 2), LBLK).astype(jnp.int32)
        is_cover = jnp.any(shuffled[:, None] == cover_ids[None, :], axis=1).astype(jnp.int32)
        reorder = jnp.argsort(is_cover, stable=True)
        remainder = shuffled[reorder][:CAP - COVER]
        return jnp.concatenate([cover_ids, remainder])
    listed = jax.vmap(one_list)(slot_keys, ranges).reshape(HEADS, N_KEYS, CAP)
    return (listed.astype(jnp.int32), counts.astype(jnp.int32))


def draw_block_ids(key, part):
    listed, counts = listed_blocks(key)
    return listed.reshape(HEADS, N_KEYS * CAP)


def draw_block_counts(key, part):
    listed, counts = listed_blocks(key)
    return counts


def draw_queries(key, part):
    base_key = jax.random.fold_in(key, 301)
    values = jax.random.truncated_normal(base_key, -4.0, 4.0, (Q_LEN, D)) * 2.5
    return values.astype(jnp.bfloat16)


def draw_key_states(key, part):
    base_key = jax.random.fold_in(key, 311)
    values = jax.random.truncated_normal(base_key, -4.0, 4.0, (CTX, D))
    return values.astype(jnp.bfloat16)


def steps_of(own_key, extent, shards, smallest, largest):
    def one(axis_at, blocks):
        draws = jax.random.uniform(jax.random.fold_in(jax.random.fold_in(own_key, 6), axis_at), (blocks,), jnp.float32, smallest / len(shards), largest / len(shards))
        return jnp.repeat(jnp.exp(draws), extent[axis_at] // blocks).reshape((-1,) + (1,) * (len(extent) - axis_at - 1))

    loudness = one(*shards[0])
    for cut in shards[1:]:
        loudness = loudness * one(*cut)
    return loudness


def normal_values(rng, extent, width, limit, pieces=(), held_as=jnp.bfloat16):
    drawn = width * jax.random.normal(rng, extent, jnp.float32)
    if pieces:
        drawn = drawn * steps_of(rng, extent, pieces, -0.22, 0.18)
    return jnp.clip(drawn, -limit, limit).astype(held_as)


def setup_inputs(seed: int = 0) -> dict:
    key_of = jax.random.split(jax.random.key(seed), 7)
    queries = draw_queries(jax.random.fold_in(key_of[6], 71), 0)
    key_states = draw_key_states(jax.random.fold_in(key_of[6], 71), 0)
    value_states = normal_values(key_of[2], (CTX, D), 1.0, 6.0, ((0, 8), (1, 4)))
    block_ids = draw_block_ids(jax.random.fold_in(key_of[6], 71), 0)
    block_counts = draw_block_counts(jax.random.fold_in(key_of[6], 71), 0)
    out_weight = normal_values(key_of[5], (D, D), D ** -0.5, 0.09375, ((0, 4),))
    return dict(queries=queries, key_states=key_states, value_states=value_states, block_ids=block_ids, block_counts=block_counts, out_weight=out_weight)


def head_attention(packed):
    query_h, key_h, value_h, ids_h, count_h = packed
    query_tile = ids_h // KTILES
    key_tile = ids_h % KTILES + (jnp.arange(N_KEYS, dtype=jnp.int32) * KTILES)[:, None]
    live_slot = jnp.arange(CAP, dtype=jnp.int32)[None, :] < count_h[:, None]
    query_blocks = query_h.astype(jnp.float32).reshape(QBLOCKS, BLOCK, HEAD_DIM)[query_tile]
    key_blocks = key_h.astype(jnp.float32).reshape(N_KEYS * KTILES, BLOCK, HEAD_DIM)[key_tile]
    value_blocks = value_h.astype(jnp.float32).reshape(N_KEYS * KTILES, BLOCK, HEAD_DIM)[key_tile]
    scores = jnp.einsum("rcid,rcjd->rcij", query_blocks, key_blocks) * (HEAD_DIM ** -0.5)
    block_best = jnp.where(live_slot[:, :, None], scores.max(-1), -jnp.inf)
    one_hot = query_tile[:, :, None] == jnp.arange(QBLOCKS, dtype=jnp.int32)[None, None, :]
    row_max = jnp.where(one_hot[..., None], block_best[:, :, None, :], -jnp.inf).max(axis=(0, 1))
    slot_max = row_max[query_tile]
    exp_terms = jnp.where(live_slot[:, :, None, None], jnp.exp(scores - slot_max[..., None]), 0.0)
    rounded = lax.optimization_barrier(exp_terms.astype(jnp.bfloat16)).astype(jnp.float32)
    value_terms = jnp.einsum("rcij,rcjd->rcid", rounded, value_blocks)
    selector = one_hot.astype(jnp.float32)
    numerator = jnp.einsum("rcq,rcid->rqid", selector, value_terms, precision=lax.Precision.HIGHEST)
    denominator = jnp.einsum("rcq,rci->rqi", selector, exp_terms.sum(-1), precision=lax.Precision.HIGHEST)
    numerator = lax.optimization_barrier(numerator.astype(jnp.bfloat16)).astype(jnp.float32).sum(0)
    denominator = lax.optimization_barrier(denominator.astype(jnp.bfloat16)).astype(jnp.float32).sum(0)
    attention = numerator / denominator[..., None]
    return attention.reshape(Q_LEN, HEAD_DIM).astype(jnp.bfloat16)


def reference(queries, key_states, value_states, block_ids, block_counts, out_weight):
    query_heads = queries.reshape(Q_LEN, HEADS, HEAD_DIM).transpose(1, 0, 2)
    key_heads = key_states.reshape(CTX, HEADS, HEAD_DIM).transpose(1, 0, 2)
    value_heads = value_states.reshape(CTX, HEADS, HEAD_DIM).transpose(1, 0, 2)
    id_table = block_ids.reshape(HEADS, N_KEYS, CAP)
    attention = lax.map(head_attention, (query_heads, key_heads, value_heads, id_table, block_counts))
    flat_rows = attention.transpose(1, 0, 2).reshape(Q_LEN, D)
    return jnp.dot(flat_rows, out_weight, preferred_element_type=jnp.float32).astype(jnp.bfloat16)
```

```python
import functools
import math

import jax
import jax.numpy as jnp
from jax import lax
from jax.experimental import pallas as pl
from jax.experimental.pallas import tpu as pltpu
from jax.sharding import PartitionSpec as P

BLOCK = 128
UNROLL = 4


def attend(unroll, tiles, coef, ids, counts, qt_ref, k_ref, v_ref, num_ref, ml_ref, acc, mx, den):
    head = pl.program_id(0)
    query_tiles = qt_ref.shape[0]
    count = counts[head]
    acc[...] = jnp.zeros_like(acc)
    den[...] = jnp.zeros_like(den)
    mx[...] = jnp.full_like(mx, -jnp.inf)

    @pl.loop(0, (count + unroll - 1) // unroll)
    def _(step):
        done = []
        for u in range(unroll):
            slot = step * unroll + u
            live = slot < count
            entry = ids[head, jnp.where(live, slot, 0)]
            query = entry // tiles
            row = pl.multiple_of((entry % tiles) * BLOCK, BLOCK)
            scores = jnp.dot(
                k_ref[pl.ds(row, BLOCK), :], qt_ref[query, 0], preferred_element_type=jnp.float32
            )
            best = scores.max(0, keepdims=True)
            terms = jnp.exp2((scores - best) * coef)
            total = terms.sum(0, keepdims=True)
            values = lax.dot_general(
                v_ref[pl.ds(row, BLOCK), :],
                terms.astype(jnp.bfloat16),
                (((0,), (0,)), ((), ())),
                preferred_element_type=jnp.float32,
            )
            done.append((jnp.where(live, query, query_tiles), best, total, values))
        for query, best, total, values in done:
            old = mx[query]
            new = jnp.maximum(old, best)
            keep = jnp.exp2((old - new) * coef)
            take = jnp.exp2((best - new) * coef)
            mx[query] = new
            den[query] = den[query] * keep + total * take
            acc[query] = acc[query] * keep + values * take

    num_ref[...] = acc[:query_tiles].astype(num_ref.dtype)[:, None]
    ml_ref[:, 0, 0:1] = mx[:query_tiles]
    ml_ref[:, 0, 1:2] = den[:query_tiles]


def partials(query_cols, key_states, value_states, ids, counts, coef):
    query_tiles, heads_here, head_dim, _ = query_cols.shape
    key_rows = key_states.shape[0]
    tiles = key_rows // BLOCK
    return pl.pallas_call(
        functools.partial(attend, UNROLL, tiles, coef),
        grid_spec=pltpu.PrefetchScalarGridSpec(
            num_scalar_prefetch=2,
            grid=(heads_here,),
            in_specs=[
                pl.BlockSpec((query_tiles, 1, head_dim, BLOCK), lambda h, *_: (0, h, 0, 0)),
                pl.BlockSpec((key_rows, head_dim), lambda h, *_: (0, h)),
                pl.BlockSpec((key_rows, head_dim), lambda h, *_: (0, h)),
            ],
            out_specs=[
                pl.BlockSpec((query_tiles, 1, head_dim, BLOCK), lambda h, *_: (0, h, 0, 0)),
                pl.BlockSpec((query_tiles, 1, 2, BLOCK), lambda h, *_: (0, h, 0, 0)),
            ],
            scratch_shapes=[
                pltpu.VMEM((query_tiles + 1, head_dim, BLOCK), jnp.float32),
                pltpu.VMEM((query_tiles + 1, 1, BLOCK), jnp.float32),
                pltpu.VMEM((query_tiles + 1, 1, BLOCK), jnp.float32),
            ],
        ),
        out_shape=[
            jax.ShapeDtypeStruct((query_tiles, heads_here, head_dim, BLOCK), jnp.bfloat16),
            jax.ShapeDtypeStruct((query_tiles, heads_here, 2, BLOCK), jnp.float32),
        ],
        compiler_params=pltpu.CompilerParams(vmem_limit_bytes=48 << 20),
        name="block_attention",
    )(ids, counts, query_cols, key_states, value_states)


def local(queries, key_states, value_states, block_ids, block_counts, out_weight):
    heads_here, _ = block_ids.shape
    head_dim = key_states.shape[1] // heads_here
    own_rows = queries.shape[0]
    own_tiles = own_rows // BLOCK
    key_groups = lax.axis_size("keys")
    coef = head_dim ** (-0.5) * math.log2(math.e)
    own_cols = queries.reshape(own_tiles, BLOCK, heads_here, head_dim).transpose(0, 2, 3, 1)
    query_cols = lax.all_gather(own_cols, "keys", axis=0, tiled=True)
    num, ml = partials(
        query_cols, key_states, value_states, block_ids, block_counts[:, 0], coef
    )
    num = lax.all_to_all(num, "keys", split_axis=0, concat_axis=0, tiled=True)
    ml = lax.all_to_all(ml, "keys", split_axis=0, concat_axis=0, tiled=True)
    num = num.reshape(key_groups, own_tiles, heads_here, head_dim, BLOCK)
    ml = ml.reshape(key_groups, own_tiles, heads_here, 2, BLOCK)
    best = ml[:, :, :, 0]
    factor = jnp.exp2((best - best.max(0)) * coef)
    weight_sum = (ml[:, :, :, 1] * factor).sum(0)
    row_sum = (num.astype(jnp.float32) * factor[:, :, :, None]).sum(0)
    attention = (row_sum / weight_sum[:, :, None]).astype(jnp.bfloat16)
    flat = attention.transpose(0, 3, 1, 2).reshape(own_rows, heads_here * head_dim)
    part = jnp.dot(flat, out_weight, preferred_element_type=jnp.float32).astype(jnp.bfloat16)
    return lax.psum_scatter(part, "heads", scatter_dimension=1, tiled=True)


def solution(mesh):
    in_specs = (
        P("keys", "heads"),
        P("keys", "heads"),
        P("keys", "heads"),
        P("heads", "keys"),
        P("heads", "keys"),
        P("heads", None),
    )
    out_specs = P("keys", "heads")
    return jax.shard_map(local, mesh=mesh, in_specs=in_specs, out_specs=out_specs, check_vma=False)
```

```python
import functools
import math

import jax
import jax.numpy as jnp
from jax import lax
from jax.experimental import pallas as pl
from jax.experimental.pallas import tpu as pltpu
from jax.sharding import PartitionSpec as P

BLOCK = 128
UNROLL = 4
MESH = pl.DeviceIdType.MESH


def attend(unroll, tiles, coef, ids, counts, qt_ref, k_ref, v_ref, num_ref, ml_ref, acc, mx, den):
    head = pl.program_id(0)
    query_tiles = qt_ref.shape[0]
    count = counts[head]
    acc[...] = jnp.zeros_like(acc)
    den[...] = jnp.zeros_like(den)
    mx[...] = jnp.full_like(mx, -jnp.inf)

    @pl.loop(0, (count + unroll - 1) // unroll)
    def _(step):
        done = []
        for u in range(unroll):
            slot = step * unroll + u
            live = slot < count
            entry = ids[head, jnp.where(live, slot, 0)]
            query = entry // tiles
            row = pl.multiple_of((entry % tiles) * BLOCK, BLOCK)
            scores = jnp.dot(
                k_ref[pl.ds(row, BLOCK), :], qt_ref[query, 0], preferred_element_type=jnp.float32
            )
            best = scores.max(0, keepdims=True)
            terms = jnp.exp2((scores - best) * coef)
            total = terms.sum(0, keepdims=True)
            values = lax.dot_general(
                v_ref[pl.ds(row, BLOCK), :],
                terms.astype(jnp.bfloat16),
                (((0,), (0,)), ((), ())),
                preferred_element_type=jnp.float32,
            )
            done.append((jnp.where(live, query, query_tiles), best, total, values))
        for query, best, total, values in done:
            old = mx[query]
            new = jnp.maximum(old, best)
            keep = jnp.exp2((old - new) * coef)
            take = jnp.exp2((best - new) * coef)
            mx[query] = new
            den[query] = den[query] * keep + total * take
            acc[query] = acc[query] * keep + values * take

    num_ref[...] = acc[:query_tiles].astype(num_ref.dtype)[:, None]
    ml_ref[:, 0, 0:1] = mx[:query_tiles]
    ml_ref[:, 0, 1:2] = den[:query_tiles]


def partials(query_cols, key_states, value_states, ids, counts, coef):
    query_tiles, heads_here, head_dim, _ = query_cols.shape
    key_rows = key_states.shape[0]
    tiles = key_rows // BLOCK
    return pl.pallas_call(
        functools.partial(attend, UNROLL, tiles, coef),
        grid_spec=pltpu.PrefetchScalarGridSpec(
            num_scalar_prefetch=2,
            grid=(heads_here,),
            in_specs=[
                pl.BlockSpec((query_tiles, 1, head_dim, BLOCK), lambda h, *_: (0, h, 0, 0)),
                pl.BlockSpec((key_rows, head_dim), lambda h, *_: (0, h)),
                pl.BlockSpec((key_rows, head_dim), lambda h, *_: (0, h)),
            ],
            out_specs=[
                pl.BlockSpec((query_tiles, 1, head_dim, BLOCK), lambda h, *_: (0, h, 0, 0)),
                pl.BlockSpec((query_tiles, 1, 2, BLOCK), lambda h, *_: (0, h, 0, 0)),
            ],
            scratch_shapes=[
                pltpu.VMEM((query_tiles + 1, head_dim, BLOCK), jnp.float32),
                pltpu.VMEM((query_tiles + 1, 1, BLOCK), jnp.float32),
                pltpu.VMEM((query_tiles + 1, 1, BLOCK), jnp.float32),
            ],
        ),
        out_shape=[
            jax.ShapeDtypeStruct((query_tiles, heads_here, head_dim, BLOCK), jnp.bfloat16),
            jax.ShapeDtypeStruct((query_tiles, heads_here, 2, BLOCK), jnp.float32),
        ],
        compiler_params=pltpu.CompilerParams(vmem_limit_bytes=48 << 20),
        name="block_attention",
    )(ids, counts, query_cols, key_states, value_states)


def everyone(sends):
    barrier = pltpu.get_barrier_semaphore()
    for device in sends:
        pl.semaphore_signal(barrier, inc=1, device_id=device, device_id_type=MESH)
    pl.semaphore_wait(barrier, len(sends))


def remote(src, dst, send_sem, recv_sem, device):
    return pltpu.make_async_remote_copy(
        src_ref=src,
        dst_ref=dst,
        send_sem=send_sem,
        recv_sem=recv_sem,
        device_id=device,
        device_id_type=MESH,
    )


def gather(pairs, q_ref, out_ref, own, own_sem, send_sem, recv_sem, pass_sem, took_sem):
    own_tiles, heads_here = own.shape[:2]
    place = lax.axis_index("keys")
    pair, core = place // 2, place % 2
    sibling = {"keys": pair * 2 + 1 - core}
    peers = [{"keys": lax.rem(pair + d, pairs) * 2 + core} for d in range(1, pairs)]
    for t in range(own_tiles):
        for h in range(heads_here):
            tile = q_ref[t * BLOCK : (t + 1) * BLOCK, h * BLOCK : (h + 1) * BLOCK]
            own[t, h] = tile.T
    everyone([sibling] + peers)
    sends, passes = [], []
    for t in range(own_tiles):
        for d in range(1, pairs):
            copy = remote(
                own.at[t],
                out_ref.at[pair, core, t],
                send_sem.at[t, d - 1],
                recv_sem.at[t, d - 1],
                peers[d - 1],
            )
            copy.start()
            sends.append((t, d, copy))
    for t in range(own_tiles):
        copy = remote(
            own.at[t],
            out_ref.at[pair, core, t],
            pass_sem.at[t, 0],
            took_sem.at[t, 0],
            sibling,
        )
        copy.start()
        passes.append(copy)
    keep = pltpu.make_async_copy(own, out_ref.at[pair, core], own_sem)
    keep.start()
    for t, d, copy in sends:
        copy.wait_recv()
        source = lax.rem(pair + pairs - d, pairs)
        block = out_ref.at[source, core, t]
        onward = remote(block, block, pass_sem.at[t, d], took_sem.at[t, d], sibling)
        onward.start()
        passes.append(onward)
    for t, d, copy in sends:
        copy.wait_send()
    keep.wait()
    for copy in passes:
        copy.wait()


def gather_queries(queries, heads_here, key_groups):
    own_tiles = queries.shape[0] // BLOCK
    pairs = key_groups // 2
    head_dim = queries.shape[1] // heads_here
    block = (own_tiles, heads_here, head_dim, BLOCK)
    out = pl.pallas_call(
        functools.partial(gather, pairs),
        in_specs=[pl.BlockSpec(memory_space=pltpu.VMEM)],
        out_specs=pl.BlockSpec(memory_space=pl.ANY),
        out_shape=jax.ShapeDtypeStruct((pairs, 2) + block, queries.dtype),
        scratch_shapes=[
            pltpu.VMEM(block, queries.dtype),
            pltpu.SemaphoreType.DMA,
            pltpu.SemaphoreType.DMA((own_tiles, pairs - 1)),
            pltpu.SemaphoreType.DMA((own_tiles, pairs - 1)),
            pltpu.SemaphoreType.DMA((own_tiles, pairs)),
            pltpu.SemaphoreType.DMA((own_tiles, pairs)),
        ],
        compiler_params=pltpu.CompilerParams(
            collective_id=0, has_side_effects=True, vmem_limit_bytes=48 << 20
        ),
        name="gather_queries",
    )(queries)
    return out.reshape((key_groups * own_tiles,) + block[1:])


def merged(parts, coef):
    best = functools.reduce(jnp.maximum, [ml[0:1] for _, ml in parts])
    shift = jnp.where(best == -jnp.inf, 0.0, best)
    factors = [jnp.exp2((ml[0:1] - shift) * coef) for _, ml in parts]
    num = sum(part.astype(jnp.float32) * f for (part, _), f in zip(parts, factors))
    den = sum(ml[1:2] * f for (_, ml), f in zip(parts, factors))
    return num, best, den


def finish(
    pairs,
    groups,
    coef,
    num_ref,
    ml_ref,
    w_ref,
    out_ref,
    weight,
    mine,
    mine_ml,
    sib,
    sib_ml,
    comb,
    comb_ml,
    got,
    got_ml,
    rows,
    part,
    kept,
    landed,
    weight_sem,
    mine_sem,
    sib_sem,
    send_sem,
    recv_sem,
    z_send,
    z_recv,
):
    own_tiles, heads_here = num_ref.shape[2:4]
    span = out_ref.shape[1]
    place, group = lax.axis_index("keys"), lax.axis_index("heads")
    pair, core = place // 2, place % 2
    sibling = {"keys": pair * 2 + 1 - core}
    peers = [{"keys": lax.rem(pair + d, pairs) * 2 + core} for d in range(1, pairs)]
    others = [{"heads": lax.rem(group + d, groups)} for d in range(1, groups)]
    load_weight = pltpu.make_async_copy(w_ref, weight, weight_sem)
    loads = []
    for t in range(own_tiles):
        loads.append(
            (
                pltpu.make_async_copy(num_ref.at[:, core, t], mine.at[t], mine_sem.at[t, 0]),
                pltpu.make_async_copy(ml_ref.at[:, core, t], mine_ml.at[t], mine_sem.at[t, 1]),
            )
        )
    everyone([sibling] + peers + others)
    swaps = []
    for t in range(own_tiles):
        swap = (
            remote(
                num_ref.at[:, 1 - core, t],
                sib.at[t],
                sib_sem.at[0, t, 0],
                sib_sem.at[1, t, 0],
                sibling,
            ),
            remote(
                ml_ref.at[:, 1 - core, t],
                sib_ml.at[t],
                sib_sem.at[0, t, 1],
                sib_sem.at[1, t, 1],
                sibling,
            ),
        )
        for copy in swap + loads[t]:
            copy.start()
        swaps.append(swap)
    load_weight.start()

    sends = []
    for t in range(own_tiles):
        for copy in loads[t]:
            copy.wait()
        for copy in swaps[t]:
            copy.wait()
        here = []
        for d in list(range(1, pairs)) + [0]:
            to = lax.rem(pair + d, pairs)

            @pl.loop(0, heads_here)
            def _(h):
                num, best, den = merged(
                    [(mine[t, to, h], mine_ml[t, to, h]), (sib[t, to, h], sib_ml[t, to, h])],
                    coef,
                )
                comb[t, d, h] = num.astype(comb.dtype)
                comb_ml[t, d, h, 0:1] = best
                comb_ml[t, d, h, 1:2] = den

            if d:
                for i, (src, dst) in enumerate([(comb, got), (comb_ml, got_ml)]):
                    copy = remote(
                        src.at[t, d],
                        dst.at[t, d - 1],
                        send_sem.at[t, d - 1, i],
                        recv_sem.at[t, d - 1, i],
                        peers[d - 1],
                    )
                    copy.start()
                    here.append(copy)
        sends.append(here)
    load_weight.wait()

    crossing = []
    for t in range(own_tiles):
        for copy in sends[t]:
            copy.wait()

        for h in range(heads_here):
            parts = [(comb[t, 0, h], comb_ml[t, 0, h])]
            parts += [(got[t, d, h], got_ml[t, d, h]) for d in range(pairs - 1)]
            num, _, den = merged(parts, coef)
            rows[:, h * BLOCK : (h + 1) * BLOCK] = (num / den).T.astype(rows.dtype)

        here = []
        for d in list(range(1, groups)) + [0]:
            start = pl.multiple_of(lax.rem(group + d, groups) * span, span)
            product = jnp.dot(
                rows[...], weight[:, pl.ds(start, span)], preferred_element_type=jnp.float32
            )
            if d:
                part[t, d - 1] = product.astype(part.dtype)
                copy = remote(
                    part.at[t, d - 1],
                    landed.at[t, d - 1],
                    z_send.at[t, d - 1],
                    z_recv.at[t, d - 1],
                    others[d - 1],
                )
                copy.start()
                here.append(copy)
            else:
                kept[t] = product
        crossing.append(here)

    for t in range(own_tiles):
        for copy in crossing[t]:
            copy.wait()
        total = kept[t]
        for d in range(groups - 1):
            total += landed[t, d].astype(jnp.float32)
        out_ref[t * BLOCK : (t + 1) * BLOCK] = total.astype(out_ref.dtype)


def finish_rows(num, ml, out_weight, coef):
    pairs, _, tiles, heads_here, head_dim, _ = num.shape
    groups = lax.axis_size("heads")
    span = out_weight.shape[1] // groups
    block = (heads_here, head_dim, BLOCK)
    small = (heads_here, 2, BLOCK)
    half, full, dma = jnp.bfloat16, jnp.float32, pltpu.SemaphoreType.DMA
    return pl.pallas_call(
        functools.partial(finish, pairs, groups, coef),
        in_specs=[pl.BlockSpec(memory_space=pl.ANY)] * 3,
        out_specs=pl.BlockSpec(memory_space=pltpu.VMEM),
        out_shape=jax.ShapeDtypeStruct((tiles * BLOCK, span), half),
        scratch_shapes=[
            pltpu.VMEM(out_weight.shape, half),
            pltpu.VMEM((tiles, pairs) + block, half),
            pltpu.VMEM((tiles, pairs) + small, full),
            pltpu.VMEM((tiles, pairs) + block, half),
            pltpu.VMEM((tiles, pairs) + small, full),
            pltpu.VMEM((tiles, pairs) + block, half),
            pltpu.VMEM((tiles, pairs) + small, full),
            pltpu.VMEM((tiles, pairs - 1) + block, half),
            pltpu.VMEM((tiles, pairs - 1) + small, full),
            pltpu.VMEM((BLOCK, heads_here * head_dim), half),
            pltpu.VMEM((tiles, groups - 1, BLOCK, span), half),
            pltpu.VMEM((tiles, BLOCK, span), full),
            pltpu.VMEM((tiles, groups - 1, BLOCK, span), half),
            dma,
            dma((tiles, 2)),
            dma((2, tiles, 2)),
            dma((tiles, pairs - 1, 2)),
            dma((tiles, pairs - 1, 2)),
            dma((tiles, groups - 1)),
            dma((tiles, groups - 1)),
        ],
        compiler_params=pltpu.CompilerParams(
            collective_id=1, has_side_effects=True, vmem_limit_bytes=56 << 20
        ),
        name="merge_and_project",
    )(num, ml, out_weight)


def local(queries, key_states, value_states, block_ids, block_counts, out_weight):
    heads_here, _ = block_ids.shape
    head_dim = key_states.shape[1] // heads_here
    key_groups = lax.axis_size("keys")
    coef = head_dim ** (-0.5) * math.log2(math.e)
    query_cols = gather_queries(queries, heads_here, key_groups)
    num, ml = partials(
        query_cols, key_states, value_states, block_ids, block_counts[:, 0], coef
    )
    shape = (key_groups // 2, 2, queries.shape[0] // BLOCK)
    num = num.reshape(shape + num.shape[1:])
    ml = ml.reshape(shape + ml.shape[1:])
    return finish_rows(num, ml, out_weight, coef)


def solution(mesh):
    in_specs = (
        P("keys", "heads"),
        P("keys", "heads"),
        P("keys", "heads"),
        P("heads", "keys"),
        P("heads", "keys"),
        P("heads", None),
    )
    out_specs = P("keys", "heads")
    return jax.shard_map(local, mesh=mesh, in_specs=in_specs, out_specs=out_specs, check_vma=False)
```

```python
import functools
import math

import jax
import jax.numpy as jnp
from jax import lax
from jax.experimental import pallas as pl
from jax.experimental.pallas import tpu as pltpu
from jax.sharding import PartitionSpec as P

BLOCK = 128
UNROLL = 8
VMEM_BYTES = 60 << 20
MESH = pl.DeviceIdType.MESH


def attend(unroll, tiles, coef, first, ids, counts, qt_ref, k_ref, v_ref, num_ref, ml_ref, acc, mx, den):
    head = first + pl.program_id(0)
    query_tiles = qt_ref.shape[0]
    count = counts[head]
    acc[...] = jnp.zeros_like(acc)
    den[...] = jnp.zeros_like(den)
    mx[...] = jnp.full_like(mx, -jnp.inf)

    @pl.loop(0, (count + unroll - 1) // unroll)
    def _(step):
        done = []
        for u in range(unroll):
            slot = step * unroll + u
            live = slot < count
            entry = ids[head, jnp.where(live, slot, 0)]
            query = entry // tiles
            row = pl.multiple_of((entry % tiles) * BLOCK, BLOCK)
            scores = jnp.dot(
                k_ref[pl.ds(row, BLOCK), :], qt_ref[query, 0], preferred_element_type=jnp.float32
            )
            best = scores.max(0, keepdims=True)
            terms = jnp.exp2((scores - best) * coef)
            total = terms.sum(0, keepdims=True)
            values = lax.dot_general(
                v_ref[pl.ds(row, BLOCK), :],
                terms.astype(jnp.bfloat16),
                (((0,), (0,)), ((), ())),
                preferred_element_type=jnp.float32,
            )
            done.append((jnp.where(live, query, query_tiles), best, total, values))
        for query, best, total, values in done:
            old = mx[query]
            new = jnp.maximum(old, best)
            keep = jnp.exp2((old - new) * coef)
            take = jnp.exp2((best - new) * coef)
            mx[query] = new
            den[query] = den[query] * keep + total * take
            acc[query] = acc[query] * keep + values * take

    num_ref[...] = acc[:query_tiles].astype(num_ref.dtype)[:, None]
    ml_ref[:, 0, 0:1] = mx[:query_tiles]
    ml_ref[:, 0, 1:2] = den[:query_tiles]


def partials(query_cols, key_states, value_states, ids, counts, coef, first):
    query_tiles, heads_here, head_dim, _ = query_cols.shape
    key_rows = key_states.shape[0]
    tiles = key_rows // BLOCK
    return pl.pallas_call(
        functools.partial(attend, UNROLL, tiles, coef, first),
        grid_spec=pltpu.PrefetchScalarGridSpec(
            num_scalar_prefetch=2,
            grid=(heads_here,),
            in_specs=[
                pl.BlockSpec((query_tiles, 1, head_dim, BLOCK), lambda h, *_: (0, h, 0, 0)),
                pl.BlockSpec((key_rows, head_dim), lambda h, *_: (0, first + h)),
                pl.BlockSpec((key_rows, head_dim), lambda h, *_: (0, first + h)),
            ],
            out_specs=[
                pl.BlockSpec((query_tiles, 1, head_dim, BLOCK), lambda h, *_: (0, h, 0, 0)),
                pl.BlockSpec((query_tiles, 1, 2, BLOCK), lambda h, *_: (0, h, 0, 0)),
            ],
            scratch_shapes=[
                pltpu.VMEM((query_tiles + 1, head_dim, BLOCK), jnp.float32),
                pltpu.VMEM((query_tiles + 1, 1, BLOCK), jnp.float32),
                pltpu.VMEM((query_tiles + 1, 1, BLOCK), jnp.float32),
            ],
        ),
        out_shape=[
            jax.ShapeDtypeStruct((query_tiles, heads_here, head_dim, BLOCK), jnp.bfloat16),
            jax.ShapeDtypeStruct((query_tiles, heads_here, 2, BLOCK), jnp.float32),
        ],
        compiler_params=pltpu.CompilerParams(vmem_limit_bytes=VMEM_BYTES),
        cost_estimate=pl.CostEstimate(
            flops=heads_here * ids.shape[1] * 4 * BLOCK**3,
            bytes_accessed=heads_here * key_rows * head_dim * 4,
            transcendentals=heads_here * ids.shape[1] * BLOCK**2,
        ),
        name="block_attention",
    )(ids, counts, query_cols, key_states, value_states)


def everyone(sends):
    barrier = pltpu.get_barrier_semaphore()
    for device in sends:
        pl.semaphore_signal(barrier, inc=1, device_id=device, device_id_type=MESH)
    pl.semaphore_wait(barrier, len(sends))


def remote(src, dst, send_sem, recv_sem, device):
    return pltpu.make_async_remote_copy(
        src_ref=src,
        dst_ref=dst,
        send_sem=send_sem,
        recv_sem=recv_sem,
        device_id=device,
        device_id_type=MESH,
    )


def gather(pairs, q_ref, out_ref, rest_ref, own, own_sem, send_sem, recv_sem, pass_sem, took_sem):
    own_tiles, heads_here = own.shape[:2]
    later_heads = rest_ref.shape[1]
    place = lax.axis_index("keys")
    pair, core = place // 2, place % 2
    sibling = {"keys": pair * 2 + 1 - core}
    peers = [{"keys": lax.rem(pair + d, pairs) * 2 + core} for d in range(1, pairs)]
    for t in range(own_tiles):
        for h in range(heads_here):
            tile = q_ref[t * BLOCK : (t + 1) * BLOCK, h * BLOCK : (h + 1) * BLOCK]
            own[t, h] = tile.T
    everyone([sibling] + peers)
    sends, passes = [], []
    for t in range(own_tiles):
        for d in range(1, pairs):
            copy = remote(
                own.at[t],
                out_ref.at[pair, core, t],
                send_sem.at[t, d - 1],
                recv_sem.at[t, d - 1],
                peers[d - 1],
            )
            copy.start()
            sends.append((t, d, copy))
    for t in range(own_tiles):
        copy = remote(
            own.at[t],
            out_ref.at[pair, core, t],
            pass_sem.at[t, 0],
            took_sem.at[t, 0],
            sibling,
        )
        copy.start()
        passes.append(copy)
    keep = pltpu.make_async_copy(own, out_ref.at[pair, core], own_sem)
    keep.start()
    for t in range(own_tiles):
        for h in range(later_heads):
            at = (heads_here + h) * BLOCK
            rest_ref[t, h] = q_ref[t * BLOCK : (t + 1) * BLOCK, at : at + BLOCK].T
    for t, d, copy in sends:
        copy.wait_recv()
        source = lax.rem(pair + pairs - d, pairs)
        block = out_ref.at[source, core, t]
        onward = remote(block, block, pass_sem.at[t, d], took_sem.at[t, d], sibling)
        onward.start()
        passes.append(onward)
    for t, d, copy in sends:
        copy.wait_send()
    keep.wait()
    for copy in passes:
        copy.wait()


def gather_queries(queries, heads_here, first_heads, key_groups):
    own_tiles = queries.shape[0] // BLOCK
    pairs = key_groups // 2
    head_dim = queries.shape[1] // heads_here
    block = (own_tiles, first_heads, head_dim, BLOCK)
    rest = (own_tiles, heads_here - first_heads, head_dim, BLOCK)
    out, later = pl.pallas_call(
        functools.partial(gather, pairs),
        in_specs=[pl.BlockSpec(memory_space=pltpu.VMEM)],
        out_specs=[pl.BlockSpec(memory_space=pl.ANY), pl.BlockSpec(memory_space=pltpu.VMEM)],
        out_shape=[
            jax.ShapeDtypeStruct((pairs, 2) + block, queries.dtype),
            jax.ShapeDtypeStruct(rest, queries.dtype),
        ],
        scratch_shapes=[
            pltpu.VMEM(block, queries.dtype),
            pltpu.SemaphoreType.DMA,
            pltpu.SemaphoreType.DMA((own_tiles, pairs - 1)),
            pltpu.SemaphoreType.DMA((own_tiles, pairs - 1)),
            pltpu.SemaphoreType.DMA((own_tiles, pairs)),
            pltpu.SemaphoreType.DMA((own_tiles, pairs)),
        ],
        compiler_params=pltpu.CompilerParams(
            collective_id=0, has_side_effects=True, vmem_limit_bytes=VMEM_BYTES
        ),
        name="gather_queries",
    )(queries)
    later = lax.all_gather(later, "keys", axis=0, tiled=True)
    return out.reshape((key_groups * own_tiles,) + block[1:]), later


def merged(parts, coef):
    best = functools.reduce(jnp.maximum, [ml[0:1] for _, ml in parts])
    shift = jnp.where(best == -jnp.inf, 0.0, best)
    factors = [jnp.exp2((ml[0:1] - shift) * coef) for _, ml in parts]
    num = sum(part.astype(jnp.float32) * f for (part, _), f in zip(parts, factors))
    den = sum(ml[1:2] * f for (_, ml), f in zip(parts, factors))
    return num, best, den


def finish(
    pairs,
    groups,
    coef,
    num_refs,
    ml_refs,
    w_ref,
    out_ref,
    weight,
    mine,
    mine_ml,
    sib,
    sib_ml,
    comb,
    comb_ml,
    got,
    got_ml,
    rows,
    part,
    kept,
    landed,
    weight_sem,
    mine_sem,
    sib_sem,
    send_sem,
    recv_sem,
    z_send,
    z_recv,
):
    own_tiles = mine.shape[0]
    heads_here = mine.shape[2]
    span = out_ref.shape[1]
    place, group = lax.axis_index("keys"), lax.axis_index("heads")
    pair, core = place // 2, place % 2
    sibling = {"keys": pair * 2 + 1 - core}
    peers = [{"keys": lax.rem(pair + d, pairs) * 2 + core} for d in range(1, pairs)]
    others = [{"heads": lax.rem(group + d, groups)} for d in range(1, groups)]
    load_weight = pltpu.make_async_copy(w_ref, weight, weight_sem)
    sources, at = [], 0
    for num_ref, ml_ref in zip(num_refs, ml_refs):
        part_heads = pl.ds(at, num_ref.shape[3])
        sources += [(num_ref, mine, sib, part_heads), (ml_ref, mine_ml, sib_ml, part_heads)]
        at += num_ref.shape[3]
    everyone([sibling] + peers + others)
    loads, swaps = [], []
    for t in range(own_tiles):
        load, swap = [], []
        for i, (src, dst, far, part_heads) in enumerate(sources):
            swap.append(
                remote(
                    src.at[:, 1 - core, t],
                    far.at[t, :, part_heads],
                    sib_sem.at[0, t, i],
                    sib_sem.at[1, t, i],
                    sibling,
                )
            )
            load.append(
                pltpu.make_async_copy(
                    src.at[:, core, t], dst.at[t, :, part_heads], mine_sem.at[t, i]
                )
            )
        for copy in swap + load:
            copy.start()
        loads.append(load)
        swaps.append(swap)
    load_weight.start()

    sends = []
    for t in range(own_tiles):
        for copy in loads[t]:
            copy.wait()
        for copy in swaps[t]:
            copy.wait()
        here = []
        for d in list(range(1, pairs)) + [0]:
            to = lax.rem(pair + d, pairs)

            @pl.loop(0, heads_here)
            def _(h):
                num, best, den = merged(
                    [(mine[t, to, h], mine_ml[t, to, h]), (sib[t, to, h], sib_ml[t, to, h])],
                    coef,
                )
                comb[t, d, h] = num.astype(comb.dtype)
                comb_ml[t, d, h, 0:1] = best
                comb_ml[t, d, h, 1:2] = den

            if d:
                for i, (src, dst) in enumerate([(comb, got), (comb_ml, got_ml)]):
                    copy = remote(
                        src.at[t, d],
                        dst.at[t, d - 1],
                        send_sem.at[t, d - 1, i],
                        recv_sem.at[t, d - 1, i],
                        peers[d - 1],
                    )
                    copy.start()
                    here.append(copy)
        sends.append(here)
    load_weight.wait()

    def hops(t, shard):
        found = []
        for way, step in enumerate((1, groups - 1)):
            copy = remote(
                part.at[way, t, shard],
                landed.at[way, t, shard],
                z_send.at[way, t, shard],
                z_recv.at[way, t, shard],
                {"heads": lax.rem(group + step, groups)},
            )
            if way == 0:
                found.append((group < shard, group > 0, copy))
            else:
                found.append((group > shard, group < groups - 1, copy))
        return found

    order = []
    for shard in range((groups + 1) // 2):
        order += [groups - 1 - shard] + [shard] * (shard != groups - 1 - shard)
    for t in range(own_tiles):
        for copy in sends[t]:
            copy.wait()

        for h in range(heads_here):
            parts = [(comb[t, 0, h], comb_ml[t, 0, h])]
            parts += [(got[t, d, h], got_ml[t, d, h]) for d in range(pairs - 1)]
            num, _, den = merged(parts, coef)
            rows[:, h * BLOCK : (h + 1) * BLOCK] = (num / den).T.astype(rows.dtype)

        for shard in order:
            kept[t, shard] = jnp.dot(
                rows[...],
                weight[:, shard * span : (shard + 1) * span],
                preferred_element_type=jnp.float32,
            )
            for way, hop in enumerate(hops(t, shard)):
                passing, inner, copy = hop

                @pl.when(passing)
                def _():
                    @pl.when(inner)
                    def _():
                        copy.wait_recv()
                        part[way, t, shard] = (
                            kept[t, shard] + landed[way, t, shard].astype(jnp.float32)
                        ).astype(part.dtype)

                    @pl.when(jnp.logical_not(inner))
                    def _():
                        part[way, t, shard] = kept[t, shard].astype(part.dtype)

                    copy.start()

    for t in range(own_tiles):
        for shard in range(groups):

            @pl.when(group == shard)
            def _():
                here = pl.ds(t * BLOCK, BLOCK)
                total = kept[t, shard]
                for way, (_, _, copy) in enumerate(hops(t, shard)):
                    if (shard > 0) if way == 0 else (shard < groups - 1):
                        copy.wait_recv()
                        total += landed[way, t, shard].astype(jnp.float32)
                out_ref[here] = total.astype(out_ref.dtype)

    for t in range(own_tiles):
        for shard in range(groups):
            for passing, _, copy in hops(t, shard):

                @pl.when(passing)
                def _():
                    copy.wait_send()


def finish_rows(nums, mls, out_weight, coef):
    pairs, _, tiles, _, head_dim, _ = nums[0].shape
    heads_here = sum(num.shape[3] for num in nums)
    groups = lax.axis_size("heads")
    span = out_weight.shape[1] // groups
    block = (heads_here, head_dim, BLOCK)
    small = (heads_here, 2, BLOCK)
    anywhere = pl.BlockSpec(memory_space=pl.ANY)
    half, full, dma = jnp.bfloat16, jnp.float32, pltpu.SemaphoreType.DMA
    return pl.pallas_call(
        functools.partial(finish, pairs, groups, coef),
        in_specs=[[anywhere] * len(nums), [anywhere] * len(mls), anywhere],
        out_specs=pl.BlockSpec(memory_space=pltpu.VMEM),
        out_shape=jax.ShapeDtypeStruct((tiles * BLOCK, span), half),
        scratch_shapes=[
            pltpu.VMEM(out_weight.shape, half),
            pltpu.VMEM((tiles, pairs) + block, half),
            pltpu.VMEM((tiles, pairs) + small, full),
            pltpu.VMEM((tiles, pairs) + block, half),
            pltpu.VMEM((tiles, pairs) + small, full),
            pltpu.VMEM((tiles, pairs) + block, half),
            pltpu.VMEM((tiles, pairs) + small, full),
            pltpu.VMEM((tiles, pairs - 1) + block, half),
            pltpu.VMEM((tiles, pairs - 1) + small, full),
            pltpu.VMEM((BLOCK, heads_here * head_dim), half),
            pltpu.VMEM((2, tiles, groups, BLOCK, span), half),
            pltpu.VMEM((tiles, groups, BLOCK, span), full),
            pltpu.VMEM((2, tiles, groups, BLOCK, span), half),
            dma,
            dma((tiles, 2 * len(nums))),
            dma((2, tiles, 2 * len(nums))),
            dma((tiles, pairs - 1, 2)),
            dma((tiles, pairs - 1, 2)),
            dma((2, tiles, groups)),
            dma((2, tiles, groups)),
        ],
        compiler_params=pltpu.CompilerParams(
            collective_id=1, has_side_effects=True, vmem_limit_bytes=VMEM_BYTES
        ),
        name="merge_and_project",
    )(nums, mls, out_weight)


def local(queries, key_states, value_states, block_ids, block_counts, out_weight):
    heads_here, _ = block_ids.shape
    head_dim = key_states.shape[1] // heads_here
    key_groups = lax.axis_size("keys")
    coef = head_dim ** (-0.5) * math.log2(math.e)
    first_heads = heads_here // 2
    gathered = gather_queries(queries, heads_here, first_heads, key_groups)
    shape = (key_groups // 2, 2, queries.shape[0] // BLOCK)
    nums, mls = [], []
    for first, query_cols in zip((0, first_heads), gathered):
        num, ml = partials(
            query_cols, key_states, value_states, block_ids, block_counts[:, 0], coef, first
        )
        nums.append(num.reshape(shape + num.shape[1:]))
        mls.append(ml.reshape(shape + ml.shape[1:]))
    return finish_rows(nums, mls, out_weight, coef)


def solution(mesh):
    in_specs = (
        P("keys", "heads"),
        P("keys", "heads"),
        P("keys", "heads"),
        P("heads", "keys"),
        P("heads", "keys"),
        P("heads", None),
    )
    out_specs = P("keys", "heads")
    return jax.shard_map(local, mesh=mesh, in_specs=in_specs, out_specs=out_specs, check_vma=False)
```

```python
import functools
import math

import jax
import jax.numpy as jnp
from jax import lax
from jax.experimental import pallas as pl
from jax.experimental.pallas import tpu as pltpu
from jax.sharding import PartitionSpec as P

BLOCK = 128
UNROLL = 8
VMEM_BYTES = 60 << 20
MESH = pl.DeviceIdType.MESH


def attend(unroll, tiles, coef, first, ids, counts, qt_ref, k_ref, v_ref, num_ref, ml_ref, acc, mx, den):
    head = first + pl.program_id(0)
    query_tiles = qt_ref.shape[0]
    count = counts[head]
    acc[...] = jnp.zeros_like(acc)
    den[...] = jnp.zeros_like(den)
    mx[...] = jnp.full_like(mx, -jnp.inf)

    @pl.loop(0, (count + unroll - 1) // unroll)
    def _(step):
        done = []
        for u in range(unroll):
            slot = step * unroll + u
            live = slot < count
            entry = ids[head, jnp.where(live, slot, 0)]
            query = entry // tiles
            row = pl.multiple_of((entry % tiles) * BLOCK, BLOCK)
            scores = jnp.dot(
                k_ref[pl.ds(row, BLOCK), :], qt_ref[query, 0], preferred_element_type=jnp.float32
            )
            best = scores.max(0, keepdims=True)
            terms = jnp.exp2((scores - best) * coef)
            total = terms.sum(0, keepdims=True)
            values = lax.dot_general(
                v_ref[pl.ds(row, BLOCK), :],
                terms.astype(jnp.bfloat16),
                (((0,), (0,)), ((), ())),
                preferred_element_type=jnp.float32,
            )
            done.append((jnp.where(live, query, query_tiles), best, total, values))
        for query, best, total, values in done:
            old = mx[query]
            new = jnp.maximum(old, best)
            keep = jnp.exp2((old - new) * coef)
            take = jnp.exp2((best - new) * coef)
            mx[query] = new
            den[query] = den[query] * keep + total * take
            acc[query] = acc[query] * keep + values * take

    num_ref[...] = acc[:query_tiles].astype(num_ref.dtype)[:, None]
    ml_ref[:, 0, 0:1] = mx[:query_tiles]
    ml_ref[:, 0, 1:2] = den[:query_tiles]


def partials(query_cols, key_states, value_states, ids, counts, coef, first):
    query_tiles, heads_here, head_dim, _ = query_cols.shape
    key_rows = key_states.shape[0]
    tiles = key_rows // BLOCK
    return pl.pallas_call(
        functools.partial(attend, UNROLL, tiles, coef, first),
        grid_spec=pltpu.PrefetchScalarGridSpec(
            num_scalar_prefetch=2,
            grid=(heads_here,),
            in_specs=[
                pl.BlockSpec((query_tiles, 1, head_dim, BLOCK), lambda h, *_: (0, h, 0, 0)),
                pl.BlockSpec((key_rows, head_dim), lambda h, *_: (0, first + h)),
                pl.BlockSpec((key_rows, head_dim), lambda h, *_: (0, first + h)),
            ],
            out_specs=[
                pl.BlockSpec((query_tiles, 1, head_dim, BLOCK), lambda h, *_: (0, h, 0, 0)),
                pl.BlockSpec((query_tiles, 1, 2, BLOCK), lambda h, *_: (0, h, 0, 0)),
            ],
            scratch_shapes=[
                pltpu.VMEM((query_tiles + 1, head_dim, BLOCK), jnp.float32),
                pltpu.VMEM((query_tiles + 1, 1, BLOCK), jnp.float32),
                pltpu.VMEM((query_tiles + 1, 1, BLOCK), jnp.float32),
            ],
        ),
        out_shape=[
            jax.ShapeDtypeStruct((query_tiles, heads_here, head_dim, BLOCK), jnp.bfloat16),
            jax.ShapeDtypeStruct((query_tiles, heads_here, 2, BLOCK), jnp.float32),
        ],
        compiler_params=pltpu.CompilerParams(vmem_limit_bytes=VMEM_BYTES),
        cost_estimate=pl.CostEstimate(
            flops=heads_here * ids.shape[1] * 4 * BLOCK**3,
            bytes_accessed=heads_here * key_rows * head_dim * 4,
            transcendentals=heads_here * ids.shape[1] * BLOCK**2,
        ),
        name="block_attention",
    )(ids, counts, query_cols, key_states, value_states)


def greet(devices):
    barrier = pltpu.get_barrier_semaphore()
    for device in devices:
        pl.semaphore_signal(barrier, inc=1, device_id=device, device_id_type=MESH)


def greeted(devices):
    pl.semaphore_wait(pltpu.get_barrier_semaphore(), len(devices))


def remote(src, dst, send_sem, recv_sem, device):
    return pltpu.make_async_remote_copy(
        src_ref=src,
        dst_ref=dst,
        send_sem=send_sem,
        recv_sem=recv_sem,
        device_id=device,
        device_id_type=MESH,
    )


def gather(pairs, q_ref, out_ref, own, own_sem, send_sem, recv_sem, pass_sem, took_sem):
    own_tiles, heads_here = own.shape[:2]
    place = lax.axis_index("keys")
    pair, core = place // 2, place % 2
    sibling = {"keys": pair * 2 + 1 - core}
    relayed = pairs == 4 and own_tiles == 2
    if relayed:
        beside = [pair + 1 - 2 * (pair % 2), lax.rem(pair + 2, pairs)]
    else:
        beside = [lax.rem(pair + d, pairs) for d in range(1, pairs)]
    peers = [{"keys": to * 2 + core} for to in beside]
    greet([sibling] + peers)

    def turn(t):
        for h in range(heads_here):
            tile = q_ref[t * BLOCK : (t + 1) * BLOCK, h * BLOCK : (h + 1) * BLOCK]
            own[t, h] = tile.T

    for t in range(own_tiles):
        turn(t)
    greeted([sibling] + peers)
    order = [(n, (t + n) % own_tiles) for t in range(own_tiles) for n in range(len(beside))]
    sends = []
    for n, t in order:
        block = out_ref.at[pair, core, t]
        copy = remote(own.at[t], block, send_sem.at[t, n], recv_sem.at[t, n], peers[n])
        copy.start()
        sends.append(copy)
    passes = []

    def onward(source, t, n):
        block = out_ref.at[source, core, t]
        src = own.at[t] if n == 0 else block
        copy = remote(src, block, pass_sem.at[t, n], took_sem.at[t, n], sibling)
        copy.start()
        passes.append(copy)

    for t in range(own_tiles):
        onward(pair, t, 0)
    keep = pltpu.make_async_copy(own, out_ref.at[pair, core], own_sem)
    keep.start()
    relays = []
    for (n, t), copy in zip(order, sends):
        copy.wait_recv()
        if relayed:
            source = beside[n]
            if t == n:
                block = out_ref.at[source, core, t]
                far = remote(block, block, send_sem.at[t, 2], recv_sem.at[t, 2], peers[1 - n])
                far.start()
                relays.append((t, far))
        else:
            source = lax.rem(pair + pairs - 1 - n, pairs)
        onward(source, t, n + 1)
    for t, copy in relays:
        copy.wait_recv()
        onward(pairs - 1 - pair, t, 3)
    for copy in sends:
        copy.wait_send()
    for _, copy in relays:
        copy.wait_send()
    keep.wait()
    for copy in passes:
        copy.wait()


def gather_queries(queries, heads_here, key_groups):
    own_tiles = queries.shape[0] // BLOCK
    pairs = key_groups // 2
    head_dim = queries.shape[1] // heads_here
    block = (own_tiles, heads_here, head_dim, BLOCK)
    dma = pltpu.SemaphoreType.DMA
    out = pl.pallas_call(
        functools.partial(gather, pairs),
        in_specs=[pl.BlockSpec(memory_space=pltpu.VMEM)],
        out_specs=pl.BlockSpec(memory_space=pl.ANY),
        out_shape=jax.ShapeDtypeStruct((pairs, 2) + block, queries.dtype),
        scratch_shapes=[
            pltpu.VMEM(block, queries.dtype),
            dma,
            dma((own_tiles, pairs - 1)),
            dma((own_tiles, pairs - 1)),
            dma((own_tiles, pairs)),
            dma((own_tiles, pairs)),
        ],
        compiler_params=pltpu.CompilerParams(
            collective_id=0, has_side_effects=True, vmem_limit_bytes=VMEM_BYTES
        ),
        name="gather_queries",
    )(queries)
    return out.reshape((key_groups * own_tiles,) + block[1:])


def merged(parts, coef):
    best = functools.reduce(jnp.maximum, [ml[0:1] for _, ml in parts])
    shift = jnp.where(best == -jnp.inf, 0.0, best)
    factors = [jnp.exp2((ml[0:1] - shift) * coef) for _, ml in parts]
    num = sum(part.astype(jnp.float32) * f for (part, _), f in zip(parts, factors))
    den = sum(ml[1:2] * f for (_, ml), f in zip(parts, factors))
    return num, best, den


def finish(
    pairs,
    groups,
    coef,
    num_refs,
    ml_refs,
    w_ref,
    out_ref,
    weight,
    mine,
    mine_ml,
    sib,
    sib_ml,
    comb,
    comb_ml,
    got,
    got_ml,
    rows,
    part,
    kept,
    landed,
    weight_sem,
    mine_sem,
    sib_sem,
    send_sem,
    recv_sem,
    z_send,
    z_recv,
):
    own_tiles = mine.shape[0]
    heads_here = mine.shape[2]
    span = out_ref.shape[1]
    place, group = lax.axis_index("keys"), lax.axis_index("heads")
    pair, core = place // 2, place % 2
    sibling = {"keys": pair * 2 + 1 - core}
    peers = [{"keys": lax.rem(pair + d, pairs) * 2 + core} for d in range(1, pairs)]
    others = [{"heads": lax.rem(group + d, groups)} for d in range(1, groups)]
    load_weight = pltpu.make_async_copy(w_ref, weight, weight_sem)
    sources, at = [], 0
    for num_ref, ml_ref in zip(num_refs, ml_refs):
        part_heads = pl.ds(at, num_ref.shape[3])
        sources += [(num_ref, mine, sib, part_heads), (ml_ref, mine_ml, sib_ml, part_heads)]
        at += num_ref.shape[3]
    greet([sibling] + peers + others)
    greeted([sibling] + peers + others)
    loads, swaps = [], []
    for t in range(own_tiles):
        load, swap = [], []
        for i, (src, dst, far, part_heads) in enumerate(sources):
            swap.append(
                remote(
                    src.at[:, 1 - core, t],
                    far.at[t, :, part_heads],
                    sib_sem.at[0, t, i],
                    sib_sem.at[1, t, i],
                    sibling,
                )
            )
            load.append(
                pltpu.make_async_copy(
                    src.at[:, core, t], dst.at[t, :, part_heads], mine_sem.at[t, i]
                )
            )
        for copy in swap + load:
            copy.start()
        loads.append(load)
        swaps.append(swap)
    load_weight.start()

    sends = []
    for t in range(own_tiles):
        for copy in loads[t]:
            copy.wait()
        for copy in swaps[t]:
            copy.wait()
        here = []
        for d in list(range(1, pairs)) + [0]:
            to = lax.rem(pair + d, pairs)

            @pl.loop(0, heads_here)
            def _(h):
                num, best, den = merged(
                    [(mine[t, to, h], mine_ml[t, to, h]), (sib[t, to, h], sib_ml[t, to, h])],
                    coef,
                )
                comb[t, d, h] = num.astype(comb.dtype)
                comb_ml[t, d, h, 0:1] = best
                comb_ml[t, d, h, 1:2] = den

            if d:
                for i, (src, dst) in enumerate([(comb, got), (comb_ml, got_ml)]):
                    copy = remote(
                        src.at[t, d],
                        dst.at[t, d - 1],
                        send_sem.at[t, d - 1, i],
                        recv_sem.at[t, d - 1, i],
                        peers[d - 1],
                    )
                    if t == 0:
                        copy.start()
                    here.append(copy)
        sends.append(here)
    load_weight.wait()

    def hops(t, shard):
        found = []
        for way, step in enumerate((1, groups - 1)):
            copy = remote(
                part.at[way, t, shard],
                landed.at[way, t, shard],
                z_send.at[way, t, shard],
                z_recv.at[way, t, shard],
                {"heads": lax.rem(group + step, groups)},
            )
            if way == 0:
                found.append((group < shard, group > 0, copy))
            else:
                found.append((group > shard, group < groups - 1, copy))
        return found

    order = []
    for shard in range((groups + 1) // 2):
        order += [groups - 1 - shard] + [shard] * (shard != groups - 1 - shard)
    for t in range(own_tiles):
        for copy in sends[t]:
            copy.wait()
        for copy in sends[t + 1] if t + 1 < own_tiles else []:
            copy.start()

        for h in range(heads_here):
            parts = [(comb[t, 0, h], comb_ml[t, 0, h])]
            parts += [(got[t, d, h], got_ml[t, d, h]) for d in range(pairs - 1)]
            num, _, den = merged(parts, coef)
            rows[:, h * BLOCK : (h + 1) * BLOCK] = (num / den).T.astype(rows.dtype)

        for shard in order:
            kept[t, shard] = jnp.dot(
                rows[...],
                weight[:, shard * span : (shard + 1) * span],
                preferred_element_type=jnp.float32,
            )
            for way, hop in enumerate(hops(t, shard)):
                passing, inner, copy = hop

                @pl.when(passing)
                def _():
                    @pl.when(inner)
                    def _():
                        copy.wait_recv()
                        part[way, t, shard] = (
                            kept[t, shard] + landed[way, t, shard].astype(jnp.float32)
                        ).astype(part.dtype)

                    @pl.when(jnp.logical_not(inner))
                    def _():
                        part[way, t, shard] = kept[t, shard].astype(part.dtype)

                    copy.start()

    for t in range(own_tiles):
        for shard in range(groups):

            @pl.when(group == shard)
            def _():
                here = pl.ds(t * BLOCK, BLOCK)
                total = kept[t, shard]
                for way, (_, _, copy) in enumerate(hops(t, shard)):
                    if (shard > 0) if way == 0 else (shard < groups - 1):
                        copy.wait_recv()
                        total += landed[way, t, shard].astype(jnp.float32)
                out_ref[here] = total.astype(out_ref.dtype)

    for t in range(own_tiles):
        for shard in range(groups):
            for passing, _, copy in hops(t, shard):

                @pl.when(passing)
                def _():
                    copy.wait_send()


def finish_rows(nums, mls, out_weight, coef):
    pairs, _, tiles, _, head_dim, _ = nums[0].shape
    heads_here = sum(num.shape[3] for num in nums)
    groups = lax.axis_size("heads")
    span = out_weight.shape[1] // groups
    block = (heads_here, head_dim, BLOCK)
    small = (heads_here, 2, BLOCK)
    anywhere = pl.BlockSpec(memory_space=pl.ANY)
    half, full, dma = jnp.bfloat16, jnp.float32, pltpu.SemaphoreType.DMA
    return pl.pallas_call(
        functools.partial(finish, pairs, groups, coef),
        in_specs=[[anywhere] * len(nums), [anywhere] * len(mls), anywhere],
        out_specs=pl.BlockSpec(memory_space=pltpu.VMEM),
        out_shape=jax.ShapeDtypeStruct((tiles * BLOCK, span), half),
        scratch_shapes=[
            pltpu.VMEM(out_weight.shape, half),
            pltpu.VMEM((tiles, pairs) + block, half),
            pltpu.VMEM((tiles, pairs) + small, full),
            pltpu.VMEM((tiles, pairs) + block, half),
            pltpu.VMEM((tiles, pairs) + small, full),
            pltpu.VMEM((tiles, pairs) + block, half),
            pltpu.VMEM((tiles, pairs) + small, full),
            pltpu.VMEM((tiles, pairs - 1) + block, half),
            pltpu.VMEM((tiles, pairs - 1) + small, full),
            pltpu.VMEM((BLOCK, heads_here * head_dim), half),
            pltpu.VMEM((2, tiles, groups, BLOCK, span), half),
            pltpu.VMEM((tiles, groups, BLOCK, span), full),
            pltpu.VMEM((2, tiles, groups, BLOCK, span), half),
            dma,
            dma((tiles, 2 * len(nums))),
            dma((2, tiles, 2 * len(nums))),
            dma((tiles, pairs - 1, 2)),
            dma((tiles, pairs - 1, 2)),
            dma((2, tiles, groups)),
            dma((2, tiles, groups)),
        ],
        compiler_params=pltpu.CompilerParams(
            collective_id=1, has_side_effects=True, vmem_limit_bytes=VMEM_BYTES
        ),
        name="merge_and_project",
    )(nums, mls, out_weight)


def local(queries, key_states, value_states, block_ids, block_counts, out_weight):
    heads_here, _ = block_ids.shape
    head_dim = key_states.shape[1] // heads_here
    key_groups = lax.axis_size("keys")
    coef = head_dim ** (-0.5) * math.log2(math.e)
    query_cols = gather_queries(queries, heads_here, key_groups)
    num, ml = partials(
        query_cols, key_states, value_states, block_ids, block_counts[:, 0], coef, 0
    )
    shape = (key_groups // 2, 2, queries.shape[0] // BLOCK)
    nums, mls = [num.reshape(shape + num.shape[1:])], [ml.reshape(shape + ml.shape[1:])]
    return finish_rows(nums, mls, out_weight, coef)


def solution(mesh):
    in_specs = (
        P("keys", "heads"),
        P("keys", "heads"),
        P("keys", "heads"),
        P("heads", "keys"),
        P("heads", "keys"),
        P("heads", None),
    )
    out_specs = P("keys", "heads")
    return jax.shard_map(local, mesh=mesh, in_specs=in_specs, out_specs=out_specs, check_vma=False)
```

```python
import functools
import math

import jax
import jax.numpy as jnp
from jax import lax
from jax.experimental import pallas as pl
from jax.experimental.pallas import tpu as pltpu
from jax.sharding import PartitionSpec as P

BLOCK = 128
UNROLL = 8
VMEM_BYTES = 60 << 20
MESH = pl.DeviceIdType.MESH


def attend(unroll, tiles, coef, first, ids, counts, qt_ref, k_ref, v_ref, num_ref, ml_ref, acc, mx, den):
    head = first + pl.program_id(0)
    query_tiles = qt_ref.shape[0]
    count = counts[head]
    acc[...] = jnp.zeros_like(acc)
    den[...] = jnp.zeros_like(den)
    mx[...] = jnp.full_like(mx, -jnp.inf)

    @pl.loop(0, (count + unroll - 1) // unroll)
    def _(step):
        done = []
        for u in range(unroll):
            slot = step * unroll + u
            live = slot < count
            entry = ids[head, jnp.where(live, slot, 0)]
            query = entry // tiles
            row = pl.multiple_of((entry % tiles) * BLOCK, BLOCK)
            scores = jnp.dot(
                k_ref[pl.ds(row, BLOCK), :], qt_ref[query, 0], preferred_element_type=jnp.float32
            )
            best = scores.max(0, keepdims=True)
            terms = jnp.exp2((scores - best) * coef)
            total = terms.sum(0, keepdims=True)
            values = lax.dot_general(
                v_ref[pl.ds(row, BLOCK), :],
                terms.astype(jnp.bfloat16),
                (((0,), (0,)), ((), ())),
                preferred_element_type=jnp.float32,
            )
            done.append((jnp.where(live, query, query_tiles), best, total, values))
        for query, best, total, values in done:
            old = mx[query]
            new = jnp.maximum(old, best)
            keep = jnp.exp2((old - new) * coef)
            take = jnp.exp2((best - new) * coef)
            mx[query] = new
            den[query] = den[query] * keep + total * take
            acc[query] = acc[query] * keep + values * take

    num_ref[...] = acc[:query_tiles].astype(num_ref.dtype)[:, None]
    ml_ref[:, 0, 0:1] = mx[:query_tiles]
    ml_ref[:, 0, 1:2] = den[:query_tiles]


def partials(query_cols, key_states, value_states, ids, counts, coef, first):
    query_tiles, heads_here, head_dim, _ = query_cols.shape
    key_rows = key_states.shape[0]
    tiles = key_rows // BLOCK
    return pl.pallas_call(
        functools.partial(attend, UNROLL, tiles, coef, first),
        grid_spec=pltpu.PrefetchScalarGridSpec(
            num_scalar_prefetch=2,
            grid=(heads_here,),
            in_specs=[
                pl.BlockSpec((query_tiles, 1, head_dim, BLOCK), lambda h, *_: (0, h, 0, 0)),
                pl.BlockSpec((key_rows, head_dim), lambda h, *_: (0, first + h)),
                pl.BlockSpec((key_rows, head_dim), lambda h, *_: (0, first + h)),
            ],
            out_specs=[
                pl.BlockSpec((query_tiles, 1, head_dim, BLOCK), lambda h, *_: (0, h, 0, 0)),
                pl.BlockSpec((query_tiles, 1, 2, BLOCK), lambda h, *_: (0, h, 0, 0)),
            ],
            scratch_shapes=[
                pltpu.VMEM((query_tiles + 1, head_dim, BLOCK), jnp.float32),
                pltpu.VMEM((query_tiles + 1, 1, BLOCK), jnp.float32),
                pltpu.VMEM((query_tiles + 1, 1, BLOCK), jnp.float32),
            ],
        ),
        out_shape=[
            jax.ShapeDtypeStruct((query_tiles, heads_here, head_dim, BLOCK), jnp.bfloat16),
            jax.ShapeDtypeStruct((query_tiles, heads_here, 2, BLOCK), jnp.float32),
        ],
        compiler_params=pltpu.CompilerParams(vmem_limit_bytes=VMEM_BYTES),
        cost_estimate=pl.CostEstimate(
            flops=heads_here * ids.shape[1] * 4 * BLOCK**3,
            bytes_accessed=heads_here * key_rows * head_dim * 4,
            transcendentals=heads_here * ids.shape[1] * BLOCK**2,
        ),
        name="block_attention",
    )(ids, counts, query_cols, key_states, value_states)


def greet(devices):
    barrier = pltpu.get_barrier_semaphore()
    for device in devices:
        pl.semaphore_signal(barrier, inc=1, device_id=device, device_id_type=MESH)


def greeted(devices):
    pl.semaphore_wait(pltpu.get_barrier_semaphore(), len(devices))


def remote(src, dst, send_sem, recv_sem, device):
    return pltpu.make_async_remote_copy(
        src_ref=src,
        dst_ref=dst,
        send_sem=send_sem,
        recv_sem=recv_sem,
        device_id=device,
        device_id_type=MESH,
    )


def gather(pairs, q_ref, out_ref, own, own_sem, send_sem, recv_sem, pass_sem, took_sem):
    own_tiles, heads_here = own.shape[:2]
    place = lax.axis_index("keys")
    pair, core = place // 2, place % 2
    sibling = {"keys": pair * 2 + 1 - core}
    relayed = pairs == 4 and own_tiles == 2
    if relayed:
        beside = [pair + 1 - 2 * (pair % 2), lax.rem(pair + 2, pairs)]
    else:
        beside = [lax.rem(pair + d, pairs) for d in range(1, pairs)]
    peers = [{"keys": to * 2 + core} for to in beside]
    greet([sibling] + peers)

    def turn(t):
        for h in range(heads_here):
            tile = q_ref[t * BLOCK : (t + 1) * BLOCK, h * BLOCK : (h + 1) * BLOCK]
            own[t, h] = tile.T

    turn(0)
    greeted([sibling] + peers)
    turned = {0}
    order = [(n, (t + n) % own_tiles) for t in range(own_tiles) for n in range(len(beside))]
    sends = []
    for n, t in order:
        if t not in turned:
            turn(t)
            turned.add(t)
        block = out_ref.at[pair, core, t]
        copy = remote(own.at[t], block, send_sem.at[t, n], recv_sem.at[t, n], peers[n])
        copy.start()
        sends.append(copy)
    passes = []

    def onward(source, t, n):
        block = out_ref.at[source, core, t]
        src = own.at[t] if n == 0 else block
        copy = remote(src, block, pass_sem.at[t, n], took_sem.at[t, n], sibling)
        copy.start()
        passes.append(copy)

    for t in range(own_tiles):
        onward(pair, t, 0)
    keep = pltpu.make_async_copy(own, out_ref.at[pair, core], own_sem)
    keep.start()
    relays = []
    for (n, t), copy in zip(order, sends):
        copy.wait_recv()
        if relayed:
            source = beside[n]
            if t == n:
                block = out_ref.at[source, core, t]
                far = remote(block, block, send_sem.at[t, 2], recv_sem.at[t, 2], peers[1 - n])
                far.start()
                relays.append((t, far))
        else:
            source = lax.rem(pair + pairs - 1 - n, pairs)
        onward(source, t, n + 1)
    for t, copy in relays:
        copy.wait_recv()
        onward(pairs - 1 - pair, t, 3)
    for copy in sends:
        copy.wait_send()
    for _, copy in relays:
        copy.wait_send()
    keep.wait()
    for copy in passes:
        copy.wait()


def gather_queries(queries, heads_here, key_groups):
    own_tiles = queries.shape[0] // BLOCK
    pairs = key_groups // 2
    head_dim = queries.shape[1] // heads_here
    block = (own_tiles, heads_here, head_dim, BLOCK)
    dma = pltpu.SemaphoreType.DMA
    out = pl.pallas_call(
        functools.partial(gather, pairs),
        in_specs=[pl.BlockSpec(memory_space=pltpu.VMEM)],
        out_specs=pl.BlockSpec(memory_space=pl.ANY),
        out_shape=jax.ShapeDtypeStruct((pairs, 2) + block, queries.dtype),
        scratch_shapes=[
            pltpu.VMEM(block, queries.dtype),
            dma,
            dma((own_tiles, pairs - 1)),
            dma((own_tiles, pairs - 1)),
            dma((own_tiles, pairs)),
            dma((own_tiles, pairs)),
        ],
        compiler_params=pltpu.CompilerParams(
            collective_id=0, has_side_effects=True, vmem_limit_bytes=VMEM_BYTES
        ),
        name="gather_queries",
    )(queries)
    return out.reshape((key_groups * own_tiles,) + block[1:])


def merged(parts, coef):
    best = functools.reduce(jnp.maximum, [ml[0:1] for _, ml in parts])
    shift = jnp.where(best == -jnp.inf, 0.0, best)
    factors = [jnp.exp2((ml[0:1] - shift) * coef) for _, ml in parts]
    num = sum(part.astype(jnp.float32) * f for (part, _), f in zip(parts, factors))
    den = sum(ml[1:2] * f for (_, ml), f in zip(parts, factors))
    return num, best, den


def finish(
    pairs,
    groups,
    coef,
    num_refs,
    ml_refs,
    w_ref,
    out_ref,
    weight,
    mine,
    mine_ml,
    sib,
    sib_ml,
    comb,
    comb_ml,
    got,
    got_ml,
    rows,
    part,
    kept,
    landed,
    weight_sem,
    mine_sem,
    sib_sem,
    send_sem,
    recv_sem,
    z_send,
    z_recv,
):
    own_tiles = mine.shape[0]
    heads_here = mine.shape[2]
    span = out_ref.shape[1]
    place, group = lax.axis_index("keys"), lax.axis_index("heads")
    pair, core = place // 2, place % 2
    sibling = {"keys": pair * 2 + 1 - core}
    peers = [{"keys": lax.rem(pair + d, pairs) * 2 + core} for d in range(1, pairs)]
    others = [{"heads": lax.rem(group + d, groups)} for d in range(1, groups)]
    load_weight = pltpu.make_async_copy(w_ref, weight, weight_sem)
    sources, at = [], 0
    for num_ref, ml_ref in zip(num_refs, ml_refs):
        part_heads = pl.ds(at, num_ref.shape[3])
        sources += [(num_ref, mine, sib, part_heads), (ml_ref, mine_ml, sib_ml, part_heads)]
        at += num_ref.shape[3]
    greet([sibling] + peers + others)
    greeted([sibling] + peers + others)
    away = list(range(1, pairs)) + [0]
    swaps = {}
    for t in range(own_tiles):
        for d in away:
            to = lax.rem(pair + d, pairs)
            swaps[t, d] = []
            for i, (src, dst, far, part_heads) in enumerate(sources):
                swaps[t, d].append(
                    remote(
                        src.at[to, 1 - core, t],
                        far.at[t, d, part_heads],
                        sib_sem.at[0, t, d, i],
                        sib_sem.at[1, t, d, i],
                        sibling,
                    )
                )
                swaps[t, d].append(
                    pltpu.make_async_copy(
                        src.at[to, core, t], dst.at[t, d, part_heads], mine_sem.at[t, d, i]
                    )
                )
    for d in away:
        for copy in swaps[0, d]:
            copy.start()
    load_weight.start()

    sends = []
    for t in range(own_tiles):
        here = []
        for d in away:
            for copy in swaps[t, d]:
                copy.wait()
            if d == 0 and t + 1 < own_tiles:
                for copy in [copy for d in away for copy in swaps[t + 1, d]]:
                    copy.start()

            @pl.loop(0, heads_here, unroll=2)
            def _(h):
                num, best, den = merged(
                    [(mine[t, d, h], mine_ml[t, d, h]), (sib[t, d, h], sib_ml[t, d, h])],
                    coef,
                )
                comb[t, d, h] = num.astype(comb.dtype)
                comb_ml[t, d, h, 0:1] = best
                comb_ml[t, d, h, 1:2] = den

            if d:
                for i, (src, dst) in enumerate([(comb, got), (comb_ml, got_ml)]):
                    copy = remote(
                        src.at[t, d],
                        dst.at[t, d - 1],
                        send_sem.at[t, d - 1, i],
                        recv_sem.at[t, d - 1, i],
                        peers[d - 1],
                    )
                    if t == 0:
                        copy.start()
                    here.append(copy)
        sends.append(here)
    load_weight.wait()

    def hops(t, shard):
        found = []
        for way, step in enumerate((1, groups - 1)):
            copy = remote(
                part.at[way, t, shard],
                landed.at[way, t, shard],
                z_send.at[way, t, shard],
                z_recv.at[way, t, shard],
                {"heads": lax.rem(group + step, groups)},
            )
            if way == 0:
                found.append((group < shard, group > 0, copy))
            else:
                found.append((group > shard, group < groups - 1, copy))
        return found

    order = []
    for shard in range((groups + 1) // 2):
        order += [groups - 1 - shard] + [shard] * (shard != groups - 1 - shard)
    for t in range(own_tiles):
        for copy in sends[t]:
            copy.wait()
        for copy in sends[t + 1] if t + 1 < own_tiles else []:
            copy.start()

        for h in range(heads_here):
            parts = [(comb[t, 0, h], comb_ml[t, 0, h])]
            parts += [(got[t, d, h], got_ml[t, d, h]) for d in range(pairs - 1)]
            num, _, den = merged(parts, coef)
            rows[:, h * BLOCK : (h + 1) * BLOCK] = (num / den).T.astype(rows.dtype)

        for shard in order:
            kept[t, shard] = jnp.dot(
                rows[...],
                weight[:, shard * span : (shard + 1) * span],
                preferred_element_type=jnp.float32,
            )
            for way, hop in enumerate(hops(t, shard)):
                passing, inner, copy = hop

                @pl.when(passing)
                def _():
                    @pl.when(inner)
                    def _():
                        copy.wait_recv()
                        part[way, t, shard] = (
                            kept[t, shard] + landed[way, t, shard].astype(jnp.float32)
                        ).astype(part.dtype)

                    @pl.when(jnp.logical_not(inner))
                    def _():
                        part[way, t, shard] = kept[t, shard].astype(part.dtype)

                    copy.start()

    for t in range(own_tiles):
        for shard in range(groups):

            @pl.when(group == shard)
            def _():
                here = pl.ds(t * BLOCK, BLOCK)
                total = kept[t, shard]
                for way, (_, _, copy) in enumerate(hops(t, shard)):
                    if (shard > 0) if way == 0 else (shard < groups - 1):
                        copy.wait_recv()
                        total += landed[way, t, shard].astype(jnp.float32)
                out_ref[here] = total.astype(out_ref.dtype)

    for t in range(own_tiles):
        for shard in range(groups):
            for passing, _, copy in hops(t, shard):

                @pl.when(passing)
                def _():
                    copy.wait_send()


def finish_rows(nums, mls, out_weight, coef):
    pairs, _, tiles, _, head_dim, _ = nums[0].shape
    heads_here = sum(num.shape[3] for num in nums)
    groups = lax.axis_size("heads")
    span = out_weight.shape[1] // groups
    block = (heads_here, head_dim, BLOCK)
    small = (heads_here, 2, BLOCK)
    anywhere = pl.BlockSpec(memory_space=pl.ANY)
    half, full, dma = jnp.bfloat16, jnp.float32, pltpu.SemaphoreType.DMA
    return pl.pallas_call(
        functools.partial(finish, pairs, groups, coef),
        in_specs=[[anywhere] * len(nums), [anywhere] * len(mls), anywhere],
        out_specs=pl.BlockSpec(memory_space=pltpu.VMEM),
        out_shape=jax.ShapeDtypeStruct((tiles * BLOCK, span), half),
        scratch_shapes=[
            pltpu.VMEM(out_weight.shape, half),
            pltpu.VMEM((tiles, pairs) + block, half),
            pltpu.VMEM((tiles, pairs) + small, full),
            pltpu.VMEM((tiles, pairs) + block, half),
            pltpu.VMEM((tiles, pairs) + small, full),
            pltpu.VMEM((tiles, pairs) + block, half),
            pltpu.VMEM((tiles, pairs) + small, full),
            pltpu.VMEM((tiles, pairs - 1) + block, half),
            pltpu.VMEM((tiles, pairs - 1) + small, full),
            pltpu.VMEM((BLOCK, heads_here * head_dim), half),
            pltpu.VMEM((2, tiles, groups, BLOCK, span), half),
            pltpu.VMEM((tiles, groups, BLOCK, span), full),
            pltpu.VMEM((2, tiles, groups, BLOCK, span), half),
            dma,
            dma((tiles, pairs, 2 * len(nums))),
            dma((2, tiles, pairs, 2 * len(nums))),
            dma((tiles, pairs - 1, 2)),
            dma((tiles, pairs - 1, 2)),
            dma((2, tiles, groups)),
            dma((2, tiles, groups)),
        ],
        compiler_params=pltpu.CompilerParams(
            collective_id=1, has_side_effects=True, vmem_limit_bytes=VMEM_BYTES
        ),
        name="merge_and_project",
    )(nums, mls, out_weight)


def local(queries, key_states, value_states, block_ids, block_counts, out_weight):
    heads_here, _ = block_ids.shape
    head_dim = key_states.shape[1] // heads_here
    key_groups = lax.axis_size("keys")
    coef = head_dim ** (-0.5) * math.log2(math.e)
    query_cols = gather_queries(queries, heads_here, key_groups)
    num, ml = partials(
        query_cols, key_states, value_states, block_ids, block_counts[:, 0], coef, 0
    )
    shape = (key_groups // 2, 2, queries.shape[0] // BLOCK)
    nums, mls = [num.reshape(shape + num.shape[1:])], [ml.reshape(shape + ml.shape[1:])]
    return finish_rows(nums, mls, out_weight, coef)


def solution(mesh):
    in_specs = (
        P("keys", "heads"),
        P("keys", "heads"),
        P("keys", "heads"),
        P("heads", "keys"),
        P("heads", "keys"),
        P("heads", None),
    )
    out_specs = P("keys", "heads")
    return jax.shard_map(local, mesh=mesh, in_specs=in_specs, out_specs=out_specs, check_vma=False)
```

```python
import functools
import math

import jax
import jax.numpy as jnp
from jax import lax
from jax.experimental import pallas as pl
from jax.experimental.pallas import tpu as pltpu
from jax.sharding import PartitionSpec as P

BLOCK = 128
UNROLL = 8
VMEM_BYTES = 60 << 20
MESH = pl.DeviceIdType.MESH


def attend(unroll, tiles, coef, first, ids, counts, qt_ref, k_ref, v_ref, num_ref, ml_ref, acc, mx, den):
    head = first + pl.program_id(0)
    query_tiles = qt_ref.shape[0]
    count = counts[head]
    acc[...] = jnp.zeros_like(acc)
    den[...] = jnp.zeros_like(den)
    mx[...] = jnp.full_like(mx, -jnp.inf)

    @pl.loop(0, (count + unroll - 1) // unroll)
    def _(step):
        seen = []
        for u in range(unroll):
            slot = step * unroll + u
            live = slot < count
            entry = ids[head, jnp.where(live, slot, 0)]
            query = entry // tiles
            row = pl.multiple_of((entry % tiles) * BLOCK, BLOCK)
            scores = jnp.dot(
                k_ref[pl.ds(row, BLOCK), :], qt_ref[query, 0], preferred_element_type=jnp.float32
            )
            best = scores.max(0, keepdims=True)
            seen.append((jnp.where(live, query, query_tiles), row, scores, best))
        done = []
        for query, row, scores, best in seen:
            old = mx[query]
            new = jnp.maximum(old, best)
            mx[query] = new
            terms = jnp.exp2((scores - new) * coef)
            values = lax.dot_general(
                v_ref[pl.ds(row, BLOCK), :],
                terms.astype(jnp.bfloat16),
                (((0,), (0,)), ((), ())),
                preferred_element_type=jnp.float32,
            )
            keep = jnp.exp2((old - new) * coef)
            done.append((query, keep, terms.sum(0, keepdims=True), values))
        for query, keep, total, values in done:
            den[query] = den[query] * keep + total
            acc[query] = acc[query] * keep + values

    num_ref[...] = acc[:query_tiles].astype(num_ref.dtype)[:, None]
    ml_ref[:, 0, 0:1] = mx[:query_tiles]
    ml_ref[:, 0, 1:2] = den[:query_tiles]


def partials(query_cols, key_states, value_states, ids, counts, coef, first):
    query_tiles, heads_here, head_dim, _ = query_cols.shape
    key_rows = key_states.shape[0]
    tiles = key_rows // BLOCK
    return pl.pallas_call(
        functools.partial(attend, UNROLL, tiles, coef, first),
        grid_spec=pltpu.PrefetchScalarGridSpec(
            num_scalar_prefetch=2,
            grid=(heads_here,),
            in_specs=[
                pl.BlockSpec((query_tiles, 1, head_dim, BLOCK), lambda h, *_: (0, h, 0, 0)),
                pl.BlockSpec((key_rows, head_dim), lambda h, *_: (0, first + h)),
                pl.BlockSpec((key_rows, head_dim), lambda h, *_: (0, first + h)),
            ],
            out_specs=[
                pl.BlockSpec((query_tiles, 1, head_dim, BLOCK), lambda h, *_: (0, h, 0, 0)),
                pl.BlockSpec((query_tiles, 1, 2, BLOCK), lambda h, *_: (0, h, 0, 0)),
            ],
            scratch_shapes=[
                pltpu.VMEM((query_tiles + 1, head_dim, BLOCK), jnp.float32),
                pltpu.VMEM((query_tiles + 1, 1, BLOCK), jnp.float32),
                pltpu.VMEM((query_tiles + 1, 1, BLOCK), jnp.float32),
            ],
        ),
        out_shape=[
            jax.ShapeDtypeStruct((query_tiles, heads_here, head_dim, BLOCK), jnp.bfloat16),
            jax.ShapeDtypeStruct((query_tiles, heads_here, 2, BLOCK), jnp.float32),
        ],
        compiler_params=pltpu.CompilerParams(vmem_limit_bytes=VMEM_BYTES),
        cost_estimate=pl.CostEstimate(
            flops=heads_here * ids.shape[1] * 4 * BLOCK**3,
            bytes_accessed=heads_here * key_rows * head_dim * 4,
            transcendentals=heads_here * ids.shape[1] * BLOCK**2,
        ),
        name="block_attention",
    )(ids, counts, query_cols, key_states, value_states)


def greet(devices):
    barrier = pltpu.get_barrier_semaphore()
    for device in devices:
        pl.semaphore_signal(barrier, inc=1, device_id=device, device_id_type=MESH)


def greeted(devices):
    pl.semaphore_wait(pltpu.get_barrier_semaphore(), len(devices))


def remote(src, dst, send_sem, recv_sem, device):
    return pltpu.make_async_remote_copy(
        src_ref=src,
        dst_ref=dst,
        send_sem=send_sem,
        recv_sem=recv_sem,
        device_id=device,
        device_id_type=MESH,
    )


def gather(pairs, q_ref, out_ref, own, own_sem, send_sem, recv_sem, pass_sem, took_sem):
    own_tiles, heads_here = own.shape[:2]
    place = lax.axis_index("keys")
    pair, core = place // 2, place % 2
    sibling = {"keys": pair * 2 + 1 - core}
    relayed = pairs == 4 and own_tiles == 2
    if relayed:
        beside = [pair + 1 - 2 * (pair % 2), lax.rem(pair + 2, pairs)]
    else:
        beside = [lax.rem(pair + d, pairs) for d in range(1, pairs)]
    peers = [{"keys": to * 2 + core} for to in beside]
    greet([sibling] + peers)

    def turn(t):
        for h in range(heads_here):
            tile = q_ref[t * BLOCK : (t + 1) * BLOCK, h * BLOCK : (h + 1) * BLOCK]
            own[t, h] = tile.T

    turn(0)
    greeted([sibling] + peers)
    turned = {0}
    order = [(n, (t + n) % own_tiles) for t in range(own_tiles) for n in range(len(beside))]
    sends = []
    for n, t in order:
        if t not in turned:
            turn(t)
            turned.add(t)
        block = out_ref.at[pair, core, t]
        copy = remote(own.at[t], block, send_sem.at[t, n], recv_sem.at[t, n], peers[n])
        copy.start()
        sends.append(copy)
    passes = []

    def onward(source, t, n):
        block = out_ref.at[source, core, t]
        src = own.at[t] if n == 0 else block
        copy = remote(src, block, pass_sem.at[t, n], took_sem.at[t, n], sibling)
        copy.start()
        passes.append(copy)

    for t in range(own_tiles):
        onward(pair, t, 0)
    keep = pltpu.make_async_copy(own, out_ref.at[pair, core], own_sem)
    keep.start()
    relays = []
    for (n, t), copy in zip(order, sends):
        copy.wait_recv()
        if relayed:
            source = beside[n]
            if t == n:
                block = out_ref.at[source, core, t]
                far = remote(block, block, send_sem.at[t, 2], recv_sem.at[t, 2], peers[1 - n])
                far.start()
                relays.append((t, far))
        else:
            source = lax.rem(pair + pairs - 1 - n, pairs)
        onward(source, t, n + 1)
    for t, copy in relays:
        copy.wait_recv()
        onward(pairs - 1 - pair, t, 3)
    for copy in sends:
        copy.wait_send()
    for _, copy in relays:
        copy.wait_send()
    keep.wait()
    for copy in passes:
        copy.wait()


def gather_queries(queries, heads_here, key_groups):
    own_tiles = queries.shape[0] // BLOCK
    pairs = key_groups // 2
    head_dim = queries.shape[1] // heads_here
    block = (own_tiles, heads_here, head_dim, BLOCK)
    dma = pltpu.SemaphoreType.DMA
    out = pl.pallas_call(
        functools.partial(gather, pairs),
        in_specs=[pl.BlockSpec(memory_space=pltpu.VMEM)],
        out_specs=pl.BlockSpec(memory_space=pl.ANY),
        out_shape=jax.ShapeDtypeStruct((pairs, 2) + block, queries.dtype),
        scratch_shapes=[
            pltpu.VMEM(block, queries.dtype),
            dma,
            dma((own_tiles, pairs - 1)),
            dma((own_tiles, pairs - 1)),
            dma((own_tiles, pairs)),
            dma((own_tiles, pairs)),
        ],
        compiler_params=pltpu.CompilerParams(
            collective_id=0, has_side_effects=True, vmem_limit_bytes=VMEM_BYTES
        ),
        name="gather_queries",
    )(queries)
    return out.reshape((key_groups * own_tiles,) + block[1:])


def merged(parts, coef):
    best = functools.reduce(jnp.maximum, [ml[0:1] for _, ml in parts])
    shift = jnp.where(best == -jnp.inf, 0.0, best)
    factors = [jnp.exp2((ml[0:1] - shift) * coef) for _, ml in parts]
    num = sum(part.astype(jnp.float32) * f for (part, _), f in zip(parts, factors))
    den = sum(ml[1:2] * f for (_, ml), f in zip(parts, factors))
    return num, best, den


def finish(
    pairs,
    groups,
    coef,
    num_refs,
    ml_refs,
    w_ref,
    out_ref,
    weight,
    mine,
    mine_ml,
    sib,
    sib_ml,
    comb,
    comb_ml,
    got,
    got_ml,
    rows,
    part,
    kept,
    landed,
    weight_sem,
    mine_sem,
    sib_sem,
    send_sem,
    recv_sem,
    z_send,
    z_recv,
):
    own_tiles = mine.shape[0]
    heads_here = mine.shape[2]
    span = out_ref.shape[1]
    place, group = lax.axis_index("keys"), lax.axis_index("heads")
    pair, core = place // 2, place % 2
    sibling = {"keys": pair * 2 + 1 - core}
    peers = [{"keys": lax.rem(pair + d, pairs) * 2 + core} for d in range(1, pairs)]
    others = [{"heads": lax.rem(group + d, groups)} for d in range(1, groups)]
    load_weight = pltpu.make_async_copy(w_ref, weight, weight_sem)
    sources, at = [], 0
    for num_ref, ml_ref in zip(num_refs, ml_refs):
        part_heads = pl.ds(at, num_ref.shape[3])
        sources += [(num_ref, mine, sib, part_heads), (ml_ref, mine_ml, sib_ml, part_heads)]
        at += num_ref.shape[3]
    greet([sibling] + peers + others)
    greeted([sibling] + peers + others)
    away = list(range(1, pairs)) + [0]
    swaps = {}
    for t in range(own_tiles):
        for d in away:
            to = lax.rem(pair + d, pairs)
            swaps[t, d] = []
            for i, (src, dst, far, part_heads) in enumerate(sources):
                swaps[t, d].append(
                    remote(
                        src.at[to, 1 - core, t],
                        far.at[t, d, part_heads],
                        sib_sem.at[0, t, d, i],
                        sib_sem.at[1, t, d, i],
                        sibling,
                    )
                )
                swaps[t, d].append(
                    pltpu.make_async_copy(
                        src.at[to, core, t], dst.at[t, d, part_heads], mine_sem.at[t, d, i]
                    )
                )
    for d in away:
        for copy in swaps[0, d]:
            copy.start()
    load_weight.start()

    sends = []
    for t in range(own_tiles):
        here = []
        for d in away:
            for copy in swaps[t, d]:
                copy.wait()
            if d == 0 and t + 1 < own_tiles:
                for copy in [copy for d in away for copy in swaps[t + 1, d]]:
                    copy.start()

            @pl.loop(0, heads_here, unroll=2)
            def _(h):
                num, best, den = merged(
                    [(mine[t, d, h], mine_ml[t, d, h]), (sib[t, d, h], sib_ml[t, d, h])],
                    coef,
                )
                comb[t, d, h] = num.astype(comb.dtype)
                comb_ml[t, d, h, 0:1] = best
                comb_ml[t, d, h, 1:2] = den

            if d:
                for i, (src, dst) in enumerate([(comb, got), (comb_ml, got_ml)]):
                    copy = remote(
                        src.at[t, d],
                        dst.at[t, d - 1],
                        send_sem.at[t, d - 1, i],
                        recv_sem.at[t, d - 1, i],
                        peers[d - 1],
                    )
                    if t == 0:
                        copy.start()
                    here.append(copy)
        sends.append(here)
    load_weight.wait()

    def hops(t, shard):
        found = []
        for way, step in enumerate((1, groups - 1)):
            copy = remote(
                part.at[way, t, shard],
                landed.at[way, t, shard],
                z_send.at[way, t, shard],
                z_recv.at[way, t, shard],
                {"heads": lax.rem(group + step, groups)},
            )
            if way == 0:
                found.append((group < shard, group > 0, copy))
            else:
                found.append((group > shard, group < groups - 1, copy))
        return found

    order = []
    for shard in range((groups + 1) // 2):
        order += [groups - 1 - shard] + [shard] * (shard != groups - 1 - shard)
    for t in range(own_tiles):
        for copy in sends[t]:
            copy.wait()
        for copy in sends[t + 1] if t + 1 < own_tiles else []:
            copy.start()

        for h in range(heads_here):
            parts = [(comb[t, 0, h], comb_ml[t, 0, h])]
            parts += [(got[t, d, h], got_ml[t, d, h]) for d in range(pairs - 1)]
            num, _, den = merged(parts, coef)
            rows[:, h * BLOCK : (h + 1) * BLOCK] = (num / den).T.astype(rows.dtype)

        for shard in order:
            kept[t, shard] = jnp.dot(
                rows[...],
                weight[:, shard * span : (shard + 1) * span],
                preferred_element_type=jnp.float32,
            )
            for way, hop in enumerate(hops(t, shard)):
                passing, inner, copy = hop

                @pl.when(passing)
                def _():
                    @pl.when(inner)
                    def _():
                        copy.wait_recv()
                        part[way, t, shard] = (
                            kept[t, shard] + landed[way, t, shard].astype(jnp.float32)
                        ).astype(part.dtype)

                    @pl.when(jnp.logical_not(inner))
                    def _():
                        part[way, t, shard] = kept[t, shard].astype(part.dtype)

                    copy.start()

    for t in range(own_tiles):
        for shard in range(groups):

            @pl.when(group == shard)
            def _():
                here = pl.ds(t * BLOCK, BLOCK)
                total = kept[t, shard]
                for way, (_, _, copy) in enumerate(hops(t, shard)):
                    if (shard > 0) if way == 0 else (shard < groups - 1):
                        copy.wait_recv()
                        total += landed[way, t, shard].astype(jnp.float32)
                out_ref[here] = total.astype(out_ref.dtype)

    for t in range(own_tiles):
        for shard in range(groups):
            for passing, _, copy in hops(t, shard):

                @pl.when(passing)
                def _():
                    copy.wait_send()


def finish_rows(nums, mls, out_weight, coef):
    pairs, _, tiles, _, head_dim, _ = nums[0].shape
    heads_here = sum(num.shape[3] for num in nums)
    groups = lax.axis_size("heads")
    span = out_weight.shape[1] // groups
    block = (heads_here, head_dim, BLOCK)
    small = (heads_here, 2, BLOCK)
    anywhere = pl.BlockSpec(memory_space=pl.ANY)
    half, full, dma = jnp.bfloat16, jnp.float32, pltpu.SemaphoreType.DMA
    return pl.pallas_call(
        functools.partial(finish, pairs, groups, coef),
        in_specs=[[anywhere] * len(nums), [anywhere] * len(mls), anywhere],
        out_specs=pl.BlockSpec(memory_space=pltpu.VMEM),
        out_shape=jax.ShapeDtypeStruct((tiles * BLOCK, span), half),
        scratch_shapes=[
            pltpu.VMEM(out_weight.shape, half),
            pltpu.VMEM((tiles, pairs) + block, half),
            pltpu.VMEM((tiles, pairs) + small, full),
            pltpu.VMEM((tiles, pairs) + block, half),
            pltpu.VMEM((tiles, pairs) + small, full),
            pltpu.VMEM((tiles, pairs) + block, half),
            pltpu.VMEM((tiles, pairs) + small, full),
            pltpu.VMEM((tiles, pairs - 1) + block, half),
            pltpu.VMEM((tiles, pairs - 1) + small, full),
            pltpu.VMEM((BLOCK, heads_here * head_dim), half),
            pltpu.VMEM((2, tiles, groups, BLOCK, span), half),
            pltpu.VMEM((tiles, groups, BLOCK, span), full),
            pltpu.VMEM((2, tiles, groups, BLOCK, span), half),
            dma,
            dma((tiles, pairs, 2 * len(nums))),
            dma((2, tiles, pairs, 2 * len(nums))),
            dma((tiles, pairs - 1, 2)),
            dma((tiles, pairs - 1, 2)),
            dma((2, tiles, groups)),
            dma((2, tiles, groups)),
        ],
        compiler_params=pltpu.CompilerParams(
            collective_id=1, has_side_effects=True, vmem_limit_bytes=VMEM_BYTES
        ),
        name="merge_and_project",
    )(nums, mls, out_weight)


def local(queries, key_states, value_states, block_ids, block_counts, out_weight):
    heads_here, _ = block_ids.shape
    head_dim = key_states.shape[1] // heads_here
    key_groups = lax.axis_size("keys")
    coef = head_dim ** (-0.5) * math.log2(math.e)
    query_cols = gather_queries(queries, heads_here, key_groups)
    num, ml = partials(
        query_cols, key_states, value_states, block_ids, block_counts[:, 0], coef, 0
    )
    shape = (key_groups // 2, 2, queries.shape[0] // BLOCK)
    nums, mls = [num.reshape(shape + num.shape[1:])], [ml.reshape(shape + ml.shape[1:])]
    return finish_rows(nums, mls, out_weight, coef)


def solution(mesh):
    in_specs = (
        P("keys", "heads"),
        P("keys", "heads"),
        P("keys", "heads"),
        P("heads", "keys"),
        P("heads", "keys"),
        P("heads", None),
    )
    out_specs = P("keys", "heads")
    return jax.shard_map(local, mesh=mesh, in_specs=in_specs, out_specs=out_specs, check_vma=False)
```

```python
import functools
import math

import jax
import jax.numpy as jnp
from jax import lax
from jax.experimental import pallas as pl
from jax.experimental.pallas import tpu as pltpu
from jax.sharding import PartitionSpec as P

BLOCK = 128
UNROLL = 6
VMEM_BYTES = 60 << 20
MESH = pl.DeviceIdType.MESH


def attend(unroll, tiles, coef, first, ids, counts, qt_ref, k_ref, v_ref, num_ref, ml_ref, acc, mx, den):
    head = first + pl.program_id(0)
    query_tiles = qt_ref.shape[0]
    count = counts[head]
    acc[...] = jnp.zeros_like(acc)
    den[...] = jnp.zeros_like(den)
    mx[...] = jnp.full_like(mx, -jnp.inf)

    @pl.loop(0, (count + unroll - 1) // unroll)
    def _(step):
        done = []
        for u in range(unroll):
            slot = step * unroll + u
            live = slot < count
            entry = ids[head, jnp.where(live, slot, 0)]
            query = entry // tiles
            row = pl.multiple_of((entry % tiles) * BLOCK, BLOCK)
            scores = jnp.dot(
                k_ref[pl.ds(row, BLOCK), :], qt_ref[query, 0], preferred_element_type=jnp.float32
            )
            best = scores.max(0, keepdims=True)
            terms = jnp.exp2((scores - best) * coef)
            total = terms.sum(0, keepdims=True)
            values = lax.dot_general(
                v_ref[pl.ds(row, BLOCK), :],
                terms.astype(jnp.bfloat16),
                (((0,), (0,)), ((), ())),
                preferred_element_type=jnp.float32,
            )
            done.append((jnp.where(live, query, query_tiles), best, total, values))
        for query, best, total, values in done:
            old = mx[query]
            new = jnp.maximum(old, best)
            keep = jnp.exp2((old - new) * coef)
            take = jnp.exp2((best - new) * coef)
            mx[query] = new
            den[query] = den[query] * keep + total * take
            acc[query] = acc[query] * keep + values * take

    num_ref[...] = acc[:query_tiles].astype(num_ref.dtype)[:, None]
    ml_ref[:, 0, 0:1] = mx[:query_tiles]
    ml_ref[:, 0, 1:2] = den[:query_tiles]


def partials(query_cols, key_states, value_states, ids, counts, coef, first):
    query_tiles, heads_here, head_dim, _ = query_cols.shape
    key_rows = key_states.shape[0]
    tiles = key_rows // BLOCK
    return pl.pallas_call(
        functools.partial(attend, UNROLL, tiles, coef, first),
        grid_spec=pltpu.PrefetchScalarGridSpec(
            num_scalar_prefetch=2,
            grid=(heads_here,),
            in_specs=[
                pl.BlockSpec((query_tiles, 1, head_dim, BLOCK), lambda h, *_: (0, h, 0, 0)),
                pl.BlockSpec((key_rows, head_dim), lambda h, *_: (0, first + h)),
                pl.BlockSpec((key_rows, head_dim), lambda h, *_: (0, first + h)),
            ],
            out_specs=[
                pl.BlockSpec((query_tiles, 1, head_dim, BLOCK), lambda h, *_: (0, h, 0, 0)),
                pl.BlockSpec((query_tiles, 1, 2, BLOCK), lambda h, *_: (0, h, 0, 0)),
            ],
            scratch_shapes=[
                pltpu.VMEM((query_tiles + 1, head_dim, BLOCK), jnp.float32),
                pltpu.VMEM((query_tiles + 1, 1, BLOCK), jnp.float32),
                pltpu.VMEM((query_tiles + 1, 1, BLOCK), jnp.float32),
            ],
        ),
        out_shape=[
            jax.ShapeDtypeStruct((query_tiles, heads_here, head_dim, BLOCK), jnp.bfloat16),
            jax.ShapeDtypeStruct((query_tiles, heads_here, 2, BLOCK), jnp.float32),
        ],
        compiler_params=pltpu.CompilerParams(vmem_limit_bytes=VMEM_BYTES),
        cost_estimate=pl.CostEstimate(
            flops=heads_here * ids.shape[1] * 4 * BLOCK**3,
            bytes_accessed=heads_here * key_rows * head_dim * 4,
            transcendentals=heads_here * ids.shape[1] * BLOCK**2,
        ),
        name="block_attention",
    )(ids, counts, query_cols, key_states, value_states)


def greet(devices):
    barrier = pltpu.get_barrier_semaphore()
    for device in devices:
        pl.semaphore_signal(barrier, inc=1, device_id=device, device_id_type=MESH)


def greeted(devices):
    pl.semaphore_wait(pltpu.get_barrier_semaphore(), len(devices))


def remote(src, dst, send_sem, recv_sem, device):
    return pltpu.make_async_remote_copy(
        src_ref=src,
        dst_ref=dst,
        send_sem=send_sem,
        recv_sem=recv_sem,
        device_id=device,
        device_id_type=MESH,
    )


def gather(pairs, q_ref, out_ref, own, own_sem, send_sem, recv_sem, pass_sem, took_sem):
    own_tiles, heads_here = own.shape[:2]
    place = lax.axis_index("keys")
    pair, core = place // 2, place % 2
    sibling = {"keys": pair * 2 + 1 - core}
    relayed = pairs == 4 and own_tiles == 2
    if relayed:
        beside = [pair + 1 - 2 * (pair % 2), lax.rem(pair + 2, pairs)]
    else:
        beside = [lax.rem(pair + d, pairs) for d in range(1, pairs)]
    peers = [{"keys": to * 2 + core} for to in beside]
    greet([sibling] + peers)

    def turn(t):
        for h in range(heads_here):
            tile = q_ref[t * BLOCK : (t + 1) * BLOCK, h * BLOCK : (h + 1) * BLOCK]
            own[t, h] = tile.T

    for t in range(own_tiles):
        turn(t)
    greeted([sibling] + peers)
    order = [(n, (t + n) % own_tiles) for t in range(own_tiles) for n in range(len(beside))]
    sends = []
    for n, t in order:
        block = out_ref.at[pair, core, t]
        copy = remote(own.at[t], block, send_sem.at[t, n], recv_sem.at[t, n], peers[n])
        copy.start()
        sends.append(copy)
    passes = []

    def onward(source, t, n):
        block = out_ref.at[source, core, t]
        src = own.at[t] if n == 0 else block
        copy = remote(src, block, pass_sem.at[t, n], took_sem.at[t, n], sibling)
        copy.start()
        passes.append(copy)

    for t in range(own_tiles):
        onward(pair, t, 0)
    keep = pltpu.make_async_copy(own, out_ref.at[pair, core], own_sem)
    keep.start()
    relays = []
    for (n, t), copy in zip(order, sends):
        copy.wait_recv()
        if relayed:
            source = beside[n]
            if t == n:
                block = out_ref.at[source, core, t]
                far = remote(block, block, send_sem.at[t, 2], recv_sem.at[t, 2], peers[1 - n])
                far.start()
                relays.append((t, far))
        else:
            source = lax.rem(pair + pairs - 1 - n, pairs)
        onward(source, t, n + 1)
    for t, copy in relays:
        copy.wait_recv()
        onward(pairs - 1 - pair, t, 3)
    for copy in sends:
        copy.wait_send()
    for _, copy in relays:
        copy.wait_send()
    keep.wait()
    for copy in passes:
        copy.wait()


def gather_queries(queries, heads_here, key_groups):
    own_tiles = queries.shape[0] // BLOCK
    pairs = key_groups // 2
    head_dim = queries.shape[1] // heads_here
    block = (own_tiles, heads_here, head_dim, BLOCK)
    dma = pltpu.SemaphoreType.DMA
    out = pl.pallas_call(
        functools.partial(gather, pairs),
        in_specs=[pl.BlockSpec(memory_space=pltpu.VMEM)],
        out_specs=pl.BlockSpec(memory_space=pl.ANY),
        out_shape=jax.ShapeDtypeStruct((pairs, 2) + block, queries.dtype),
        scratch_shapes=[
            pltpu.VMEM(block, queries.dtype),
            dma,
            dma((own_tiles, pairs - 1)),
            dma((own_tiles, pairs - 1)),
            dma((own_tiles, pairs)),
            dma((own_tiles, pairs)),
        ],
        compiler_params=pltpu.CompilerParams(
            collective_id=0, has_side_effects=True, vmem_limit_bytes=VMEM_BYTES
        ),
        name="gather_queries",
    )(queries)
    return out.reshape((key_groups * own_tiles,) + block[1:])


def merged(parts, coef):
    best = functools.reduce(jnp.maximum, [ml[0:1] for _, ml in parts])
    shift = jnp.where(best == -jnp.inf, 0.0, best)
    factors = [jnp.exp2((ml[0:1] - shift) * coef) for _, ml in parts]
    num = sum(part.astype(jnp.float32) * f for (part, _), f in zip(parts, factors))
    den = sum(ml[1:2] * f for (_, ml), f in zip(parts, factors))
    return num, best, den


def finish(
    pairs,
    groups,
    coef,
    num_refs,
    ml_refs,
    w_ref,
    out_ref,
    weight,
    mine,
    mine_ml,
    sib,
    sib_ml,
    comb,
    comb_ml,
    got,
    got_ml,
    rows,
    part,
    kept,
    landed,
    weight_sem,
    mine_sem,
    sib_sem,
    send_sem,
    recv_sem,
    z_send,
    z_recv,
):
    own_tiles = mine.shape[0]
    heads_here = mine.shape[2]
    span = out_ref.shape[1]
    place, group = lax.axis_index("keys"), lax.axis_index("heads")
    pair, core = place // 2, place % 2
    sibling = {"keys": pair * 2 + 1 - core}
    peers = [{"keys": lax.rem(pair + d, pairs) * 2 + core} for d in range(1, pairs)]
    others = [{"heads": lax.rem(group + d, groups)} for d in range(1, groups)]
    load_weight = pltpu.make_async_copy(w_ref, weight, weight_sem)
    sources, at = [], 0
    for num_ref, ml_ref in zip(num_refs, ml_refs):
        part_heads = pl.ds(at, num_ref.shape[3])
        sources += [(num_ref, mine, sib, part_heads), (ml_ref, mine_ml, sib_ml, part_heads)]
        at += num_ref.shape[3]
    greet([sibling] + peers + others)
    greeted([sibling] + peers + others)
    loads, swaps = [], []
    for t in range(own_tiles):
        load, swap = [], []
        for i, (src, dst, far, part_heads) in enumerate(sources):
            swap.append(
                remote(
                    src.at[:, 1 - core, t],
                    far.at[t, :, part_heads],
                    sib_sem.at[0, t, i],
                    sib_sem.at[1, t, i],
                    sibling,
                )
            )
            load.append(
                pltpu.make_async_copy(
                    src.at[:, core, t], dst.at[t, :, part_heads], mine_sem.at[t, i]
                )
            )
        for copy in swap + load:
            copy.start()
        loads.append(load)
        swaps.append(swap)
    load_weight.start()

    sends = []
    for t in range(own_tiles):
        for copy in loads[t]:
            copy.wait()
        for copy in swaps[t]:
            copy.wait()
        here = []
        for d in list(range(1, pairs)) + [0]:
            to = lax.rem(pair + d, pairs)

            @pl.loop(0, heads_here)
            def _(h):
                num, best, den = merged(
                    [(mine[t, to, h], mine_ml[t, to, h]), (sib[t, to, h], sib_ml[t, to, h])],
                    coef,
                )
                comb[t, d, h] = num.astype(comb.dtype)
                comb_ml[t, d, h, 0:1] = best
                comb_ml[t, d, h, 1:2] = den

            if d:
                for i, (src, dst) in enumerate([(comb, got), (comb_ml, got_ml)]):
                    copy = remote(
                        src.at[t, d],
                        dst.at[t, d - 1],
                        send_sem.at[t, d - 1, i],
                        recv_sem.at[t, d - 1, i],
                        peers[d - 1],
                    )
                    if t == 0:
                        copy.start()
                    here.append(copy)
        sends.append(here)
    load_weight.wait()

    def hops(t, shard):
        found = []
        for way, step in enumerate((1, groups - 1)):
            copy = remote(
                part.at[way, t, shard],
                landed.at[way, t, shard],
                z_send.at[way, t, shard],
                z_recv.at[way, t, shard],
                {"heads": lax.rem(group + step, groups)},
            )
            if way == 0:
                found.append((group < shard, group > 0, copy))
            else:
                found.append((group > shard, group < groups - 1, copy))
        return found

    order = []
    for shard in range((groups + 1) // 2):
        order += [groups - 1 - shard] + [shard] * (shard != groups - 1 - shard)
    for t in range(own_tiles):
        for copy in sends[t]:
            copy.wait()
        for copy in sends[t + 1] if t + 1 < own_tiles else []:
            copy.start()

        for h in range(heads_here):
            parts = [(comb[t, 0, h], comb_ml[t, 0, h])]
            parts += [(got[t, d, h], got_ml[t, d, h]) for d in range(pairs - 1)]
            num, _, den = merged(parts, coef)
            rows[:, h * BLOCK : (h + 1) * BLOCK] = (num / den).T.astype(rows.dtype)

        for shard in order:
            kept[t, shard] = jnp.dot(
                rows[...],
                weight[:, shard * span : (shard + 1) * span],
                preferred_element_type=jnp.float32,
            )
            for way, hop in enumerate(hops(t, shard)):
                passing, inner, copy = hop

                @pl.when(passing)
                def _():
                    @pl.when(inner)
                    def _():
                        copy.wait_recv()
                        part[way, t, shard] = (
                            kept[t, shard] + landed[way, t, shard].astype(jnp.float32)
                        ).astype(part.dtype)

                    @pl.when(jnp.logical_not(inner))
                    def _():
                        part[way, t, shard] = kept[t, shard].astype(part.dtype)

                    copy.start()

    for t in range(own_tiles):
        for shard in range(groups):

            @pl.when(group == shard)
            def _():
                here = pl.ds(t * BLOCK, BLOCK)
                total = kept[t, shard]
                for way, (_, _, copy) in enumerate(hops(t, shard)):
                    if (shard > 0) if way == 0 else (shard < groups - 1):
                        copy.wait_recv()
                        total += landed[way, t, shard].astype(jnp.float32)
                out_ref[here] = total.astype(out_ref.dtype)

    for t in range(own_tiles):
        for shard in range(groups):
            for passing, _, copy in hops(t, shard):

                @pl.when(passing)
                def _():
                    copy.wait_send()


def finish_rows(nums, mls, out_weight, coef):
    pairs, _, tiles, _, head_dim, _ = nums[0].shape
    heads_here = sum(num.shape[3] for num in nums)
    groups = lax.axis_size("heads")
    span = out_weight.shape[1] // groups
    block = (heads_here, head_dim, BLOCK)
    small = (heads_here, 2, BLOCK)
    anywhere = pl.BlockSpec(memory_space=pl.ANY)
    half, full, dma = jnp.bfloat16, jnp.float32, pltpu.SemaphoreType.DMA
    return pl.pallas_call(
        functools.partial(finish, pairs, groups, coef),
        in_specs=[[anywhere] * len(nums), [anywhere] * len(mls), anywhere],
        out_specs=pl.BlockSpec(memory_space=pltpu.VMEM),
        out_shape=jax.ShapeDtypeStruct((tiles * BLOCK, span), half),
        scratch_shapes=[
            pltpu.VMEM(out_weight.shape, half),
            pltpu.VMEM((tiles, pairs) + block, half),
            pltpu.VMEM((tiles, pairs) + small, full),
            pltpu.VMEM((tiles, pairs) + block, half),
            pltpu.VMEM((tiles, pairs) + small, full),
            pltpu.VMEM((tiles, pairs) + block, half),
            pltpu.VMEM((tiles, pairs) + small, full),
            pltpu.VMEM((tiles, pairs - 1) + block, half),
            pltpu.VMEM((tiles, pairs - 1) + small, full),
            pltpu.VMEM((BLOCK, heads_here * head_dim), half),
            pltpu.VMEM((2, tiles, groups, BLOCK, span), half),
            pltpu.VMEM((tiles, groups, BLOCK, span), full),
            pltpu.VMEM((2, tiles, groups, BLOCK, span), half),
            dma,
            dma((tiles, 2 * len(nums))),
            dma((2, tiles, 2 * len(nums))),
            dma((tiles, pairs - 1, 2)),
            dma((tiles, pairs - 1, 2)),
            dma((2, tiles, groups)),
            dma((2, tiles, groups)),
        ],
        compiler_params=pltpu.CompilerParams(
            collective_id=1, has_side_effects=True, vmem_limit_bytes=VMEM_BYTES
        ),
        name="merge_and_project",
    )(nums, mls, out_weight)


def local(queries, key_states, value_states, block_ids, block_counts, out_weight):
    heads_here, _ = block_ids.shape
    head_dim = key_states.shape[1] // heads_here
    key_groups = lax.axis_size("keys")
    coef = head_dim ** (-0.5) * math.log2(math.e)
    query_cols = gather_queries(queries, heads_here, key_groups)
    num, ml = partials(
        query_cols, key_states, value_states, block_ids, block_counts[:, 0], coef, 0
    )
    shape = (key_groups // 2, 2, queries.shape[0] // BLOCK)
    nums, mls = [num.reshape(shape + num.shape[1:])], [ml.reshape(shape + ml.shape[1:])]
    return finish_rows(nums, mls, out_weight, coef)


def solution(mesh):
    in_specs = (
        P("keys", "heads"),
        P("keys", "heads"),
        P("keys", "heads"),
        P("heads", "keys"),
        P("heads", "keys"),
        P("heads", None),
    )
    out_specs = P("keys", "heads")
    return jax.shard_map(local, mesh=mesh, in_specs=in_specs, out_specs=out_specs, check_vma=False)
```
